32 devices in a mesh: expert: 8 (over z, y), fsdp: 4 (over x, core).
Axes of the slice: x: 2, y: 2, z: 4, core: 2. Of those that a mesh axis runs over, the one named last changes fastest.
Arguments:
- feats: bfloat16 [128, 128, 1536], P('expert', None, 'fsdp'), may hold values from -6 to 6
- cotan: bfloat16 [128, 128, 1536], P('expert', None, 'fsdp'), may hold values from -6 to 6
- lang: int32 [128], P('expert'), may hold values from 0 to 7, as said below
- w_out: bfloat16 [8, 1536, 1536], P('expert', 'fsdp'), may hold values from -0.15625 to 0.15625
- gain: bfloat16 [8, 1536], P('expert', 'fsdp'), may hold values from 0.099609375 to 1.8984375
- kernel: bfloat16 [8, 31, 1536], P('expert', None, 'fsdp'), may hold values from -1 to 1
Outputs:
- feat_grad: bfloat16 [128, 128, 1536], P('expert', None, 'fsdp')
- w_grad: bfloat16 [8, 1536, 1536], P('expert', 'fsdp')
- gain_grad: float32 [8, 1536], P('expert', 'fsdp')
- kernel_grad: float32 [8, 31, 1536], P('expert', None, 'fsdp')
The draws below stay inside these ranges and needn't reach their ends.
Inputs may be any that keep to these rules, and one draw needn't show every extreme that they name: `lang`: each index of the expert axis holds either none or exactly 4 segments of a language, and each language has exactly 16 segments in all.
All inputs are finite; a program needn't handle non-finite values.
Results may differ from the reference program's by a relative error of at most 0.005.
Values may be sent and summed in bfloat16 or wider, within the bound.
No kernel may reach another device: no remote copies, remote signals or barrier semaphores. Data moves between devices by JAX's collectives and lax.ppermute only.
A program may use at most 128 MiB of HBM per device.

```python
import jax
import jax.numpy as jnp
from jax import lax

D = 1536
KERNEL = 31
FRAMES = 128
SEGS = 16
CAP = 4
SEG_COL = 128
N_EXPERT = 8


def draw_lang(key, part):
    first_key, second_key = jax.random.split(key, 2)
    col_keys = jax.random.randint(first_key, (N_EXPERT,), 0, 1 << 20)
    perms = jnp.argsort(col_keys * N_EXPERT + jnp.arange(N_EXPERT)).astype(jnp.int32)
    seg_keys = jax.random.randint(second_key, (N_EXPERT, SEGS), 0, 1 << 20)
    shuffles = jnp.argsort(seg_keys * SEGS + jnp.arange(SEGS)[None, :], axis=1).astype(jnp.int32)
    group_index = shuffles // CAP
    source = jnp.arange(N_EXPERT, dtype=jnp.int32)[:, None]
    residue = (source * (SEGS // CAP) + group_index) % N_EXPERT
    language = perms[residue.reshape(N_EXPERT * SEGS)]
    return language.astype(jnp.int32)


def levels(key, extent, cuts, least, largest):
    loudness = 1.0
    for dim, shards_of in cuts:
        steps = jax.random.uniform(jax.random.fold_in(jax.random.fold_in(key, 6), dim), (shards_of,), jnp.float32, least / len(cuts), largest / len(cuts))
        loudness = loudness * jnp.repeat(jnp.exp(steps), extent[dim] // shards_of).reshape((-1,) + (1,) * (len(extent) - 1 - dim))
    return loudness


def normal_values(stream_key, shape, scale, reach, cuts=(), held_as=jnp.bfloat16):
    drawn = jax.random.normal(stream_key, shape, jnp.float32) * scale
    if len(cuts) > 0:
        drawn = levels(stream_key, shape, cuts, -0.22, 0.18) * drawn
    return jnp.clip(drawn, min=-reach, max=reach).astype(held_as)


def setup_inputs(seed: int = 0) -> dict:
    seeds = jax.random.split(jax.random.key(seed), 7)
    return {
        "feats": normal_values(seeds[0], (SEG_COL, FRAMES, D), 1.0, 6.0, ((0, 8), (2, 4))),
        "cotan": normal_values(seeds[1], (SEG_COL, FRAMES, D), 1.0, 6.0, ((0, 8), (2, 4))),
        "lang": draw_lang(jax.random.fold_in(seeds[6], 71), 0),
        "w_out": normal_values(seeds[3], (N_EXPERT, D, D), D ** -0.5, 0.15625, ((0, 8), (1, 4))),
        "gain": jnp.clip(1.0 + 0.18 * jax.random.normal(seeds[4], (N_EXPERT, D), jnp.float32), 0.099609375, 1.8984375).astype(jnp.bfloat16),
        "kernel": normal_values(seeds[5], (N_EXPERT, KERNEL, D), KERNEL ** -0.5, 1.0, ((0, 8), (2, 4))),
    }


def front(inputs, norm_gain, conv_taps):
    values = inputs.astype(jnp.float32)
    centre = values - lax.optimization_barrier(jnp.mean(values, axis=-1, keepdims=True))
    inv_std = lax.rsqrt(lax.optimization_barrier(jnp.mean(centre * centre, axis=-1, keepdims=True)) + 1e-05)
    normed = centre * inv_std
    scaled = normed * norm_gain
    tap_count = conv_taps.shape[0]
    half_width = tap_count // 2
    frames = inputs.shape[1]
    padded = jnp.pad(scaled, ((0, 0), (half_width, half_width), (0, 0)))
    conv_out = jnp.zeros_like(scaled)
    for offset in range(tap_count):
        conv_out = conv_out + conv_taps[offset] * padded[:, offset:offset + frames]
    gate_sig = jax.nn.sigmoid(conv_out)
    hidden = (conv_out * gate_sig).astype(jnp.bfloat16)
    return (normed, inv_std, padded, conv_out, gate_sig, hidden)

def back(hid_grad, grads_in, normed, inv_std, padded, conv_out, gate_sig, norm_gain, conv_taps):
    tap_count = conv_taps.shape[0]
    half_width = tap_count // 2
    frames = normed.shape[1]
    conv_grad = hid_grad * gate_sig * (1.0 + conv_out * (1.0 - gate_sig))
    grad_padded = jnp.pad(conv_grad, ((0, 0), (half_width, half_width), (0, 0)))
    scaled_grad = jnp.zeros_like(conv_grad)
    tap_grads = []
    for offset in range(tap_count):
        first_row = 2 * half_width - offset
        scaled_grad = scaled_grad + conv_taps[offset] * grad_padded[:, first_row:first_row + frames]
        tap_grads.append(lax.optimization_barrier(jnp.sum(conv_grad * padded[:, offset:offset + frames], axis=(0, 1))))
    gain_grad = lax.optimization_barrier(jnp.sum(scaled_grad * normed, axis=(0, 1)))
    norm_grad = scaled_grad * norm_gain
    branch = inv_std * (norm_grad - lax.optimization_barrier(jnp.mean(norm_grad, axis=-1, keepdims=True)) - normed * lax.optimization_barrier(jnp.mean(norm_grad * normed, axis=-1, keepdims=True)))
    input_grad = (grads_in.astype(jnp.float32) + branch).astype(jnp.bfloat16)
    return (input_grad, gain_grad, jnp.stack(tap_grads))

def reference(feats, cotan, lang, w_out, gain, kernel):
    orders = jnp.argsort(lang, stable=True).astype(jnp.int32)
    grouped = orders.reshape(N_EXPERT, SEGS)
    grad_scale = float(SEGS * FRAMES) ** (-0.5)

    def per_expert(operands):
        rows_e, weight_e, gain_e, taps_e = operands
        xs_e = feats[rows_e]
        dys_e = cotan[rows_e]
        norm_gain = gain_e.astype(jnp.float32)
        conv_taps = taps_e.astype(jnp.float32)
        normed, inv_std, padded, conv_out, gate_sig, hidden = front(xs_e, norm_gain, conv_taps)
        dy_rows = dys_e.reshape(-1, D)
        hid_grad = jnp.dot(dy_rows, weight_e.T, preferred_element_type=jnp.float32).reshape(normed.shape)
        input_grad, gain_grad, tap_grad = back(hid_grad, dys_e, normed, inv_std, padded, conv_out, gate_sig, norm_gain, conv_taps)
        weight_grad = jnp.dot(hidden.reshape(-1, D).T, dy_rows, preferred_element_type=jnp.float32) * grad_scale
        return (input_grad, weight_grad.astype(jnp.bfloat16), gain_grad * grad_scale, tap_grad * grad_scale)
    grads_sorted, w_grad, gain_grad, kernel_grad = lax.map(per_expert, (grouped, w_out, gain, kernel))
    inverse = jnp.argsort(orders).astype(jnp.int32)
    feat_grad = grads_sorted.reshape(N_EXPERT * SEGS, FRAMES, D)[inverse]
    return (feat_grad, w_grad, gain_grad, kernel_grad)
```

```python
import math

import jax
import jax.numpy as jnp
import ml_dtypes
import numpy as np
from jax import lax
from jax.experimental import pallas as pl
from jax.experimental.pallas import tpu as pltpu
from jax.sharding import PartitionSpec as P

BF16 = jnp.bfloat16
F32 = jnp.float32
MIB = 1024 * 1024

def normalize(values, feature_total):
    value_sum = lax.psum(jnp.sum(values, axis=-1), "fsdp")
    centre = values - (value_sum / feature_total)[..., None]
    square_sum = lax.psum(jnp.sum(centre * centre, axis=-1), "fsdp")
    row_var = square_sum / feature_total
    inv_std = lax.rsqrt(row_var + 1e-05)[..., None]
    return (centre * inv_std, inv_std)


def forward_part(inputs, norm_gain, conv_taps, feature_total):
    normed, inv_std = normalize(inputs.astype(jnp.float32), feature_total)
    scaled = normed * norm_gain
    tap_count = conv_taps.shape[0]
    half_width = tap_count // 2
    frames = inputs.shape[1]
    padded = jnp.pad(scaled, ((0, 0), (half_width, half_width), (0, 0)))
    conv_out = jnp.zeros_like(scaled)
    for offset in range(tap_count):
        conv_out = conv_out + conv_taps[offset] * padded[:, offset : offset + frames]
    gate_sig = jax.nn.sigmoid(conv_out)
    hidden = (conv_out * gate_sig).astype(jnp.bfloat16)
    return (normed, inv_std, padded, conv_out, gate_sig, hidden)


def back_split(
    hid_grad,
    grads_in,
    normed,
    inv_std,
    padded,
    conv_out,
    gate_sig,
    norm_gain,
    conv_taps,
    feature_total,
):
    tap_count = conv_taps.shape[0]
    half_width = tap_count // 2
    frames = normed.shape[1]
    conv_grad = hid_grad * gate_sig * (1.0 + conv_out * (1.0 - gate_sig))
    grad_padded = jnp.pad(conv_grad, ((0, 0), (half_width, half_width), (0, 0)))
    scaled_grad = jnp.zeros_like(conv_grad)
    tap_grads = []
    for offset in range(tap_count):
        first_row = 2 * half_width - offset
        scaled_grad = (
            scaled_grad + conv_taps[offset] * grad_padded[:, first_row : first_row + frames]
        )
        tap_grads.append(jnp.sum(conv_grad * padded[:, offset : offset + frames], axis=(0, 1)))
    gain_grad = jnp.sum(scaled_grad * normed, axis=(0, 1))
    norm_grad = scaled_grad * norm_gain
    grad_total, cross_total = lax.psum(
        (jnp.sum(norm_grad, axis=-1), jnp.sum(norm_grad * normed, axis=-1)), "fsdp"
    )
    branch = inv_std * (
        norm_grad
        - (grad_total / feature_total)[..., None]
        - normed * (cross_total / feature_total)[..., None]
    )
    input_grad = (grads_in.astype(jnp.float32) + branch).astype(jnp.bfloat16)
    return (input_grad, gain_grad, jnp.stack(tap_grads))


def arrival_map(recv_occupied, seg_count):
    flat_occupied = recv_occupied.reshape(-1)
    order_pos = jnp.cumsum(flat_occupied) - 1
    position = jnp.arange(seg_count, dtype=jnp.int32)
    return ((order_pos[None, :] == position[:, None]) & (flat_occupied[None, :] > 0)).astype(
        jnp.bfloat16
    )


def compact_rows(compact_map, received, row_shape):
    flat = received.reshape(compact_map.shape[1], -1)
    return (
        jnp.dot(compact_map, flat, preferred_element_type=jnp.float32)
        .astype(jnp.bfloat16)
        .reshape(row_shape)
    )


def routed_frames(feats, cotan, lang, w_out, gain, kernel):
    seg_count, frames, part_width = feats.shape
    owners = lax.axis_size("expert")
    feature_total = part_width * lax.axis_size("fsdp")
    capacity = max(1, 2 * seg_count // owners)
    slot_count = owners * capacity
    position = jnp.arange(seg_count, dtype=jnp.int32)
    earlier_same = (lang[:, None] == lang[None, :]) & (position[:, None] < position[None, :])
    slot_rank = jnp.sum(earlier_same.astype(jnp.int32), axis=0)
    slot_of = lang * capacity + slot_rank
    routing = jnp.arange(slot_count, dtype=jnp.int32)[:, None] == slot_of[None, :]
    routing_b = routing.astype(jnp.bfloat16)
    send_x = (
        jnp.dot(routing_b, feats.reshape(seg_count, -1), preferred_element_type=jnp.float32)
        .astype(jnp.bfloat16)
        .reshape(owners, capacity, -1)
    )
    send_dy = (
        jnp.dot(routing_b, cotan.reshape(seg_count, -1), preferred_element_type=jnp.float32)
        .astype(jnp.bfloat16)
        .reshape(owners, capacity, -1)
    )
    occupied = jnp.sum(routing.astype(jnp.int32), axis=1).reshape(owners, capacity)
    norm_gain = gain[0].astype(jnp.float32)
    conv_taps = kernel[0].astype(jnp.float32)
    row_shape = (seg_count, frames, part_width)
    recv_x, recv_dy, recv_occupied = (
        lax.all_to_all(send_x, "expert", split_axis=0, concat_axis=0, tiled=True),
        lax.all_to_all(send_dy, "expert", split_axis=0, concat_axis=0, tiled=True),
        lax.all_to_all(occupied, "expert", split_axis=0, concat_axis=0, tiled=True),
    )
    compact_map = arrival_map(recv_occupied, seg_count)
    own_x = compact_rows(compact_map, recv_x, row_shape)
    forward = forward_part(own_x, norm_gain, conv_taps, feature_total)
    own_dy = compact_rows(compact_map, recv_dy, row_shape)
    normed, inv_std, padded, conv_out, gate_sig, hidden = forward
    grad_scale = float(seg_count * frames) ** (-0.5)
    hidden_rows = hidden.reshape(-1, part_width)
    w_rows = w_out[0]
    shard_part = lax.all_gather(own_dy.reshape(-1, part_width), "fsdp", axis=1, tiled=True)
    hid_sum = jnp.dot(shard_part, w_rows.T, preferred_element_type=jnp.float32)
    w_block = jnp.dot(hidden_rows.T, shard_part, preferred_element_type=jnp.float32) * grad_scale
    w_sum = w_block
    hid_sum, w_sum = (hid_sum, w_sum)
    hid_grad = hid_sum.reshape(row_shape)
    input_grad, gain_grad, tap_grad = back_split(
        hid_grad,
        own_dy,
        normed,
        inv_std,
        padded,
        conv_out,
        gate_sig,
        norm_gain,
        conv_taps,
        feature_total,
    )
    back_slots = jnp.dot(
        compact_map.T, input_grad.reshape(seg_count, -1), preferred_element_type=jnp.float32
    ).astype(jnp.bfloat16)
    home_slots = lax.all_to_all(
        back_slots.reshape(owners, capacity, -1), "expert", split_axis=0, concat_axis=0, tiled=True
    )
    feat_grad = (
        jnp.dot(routing_b.T, home_slots.reshape(slot_count, -1), preferred_element_type=jnp.float32)
        .astype(jnp.bfloat16)
        .reshape(feats.shape)
    )
    return (
        feat_grad,
        w_sum.astype(jnp.bfloat16)[None],
        (gain_grad * grad_scale)[None],
        (tap_grad * grad_scale)[None],
    )


def split_const(matrix):
    high = matrix.astype(ml_dtypes.bfloat16)
    low = (matrix - high.astype(np.float64)).astype(ml_dtypes.bfloat16)
    return np.concatenate([high, high, low], axis=1)


def wave_tables(frames, taps):
    half = taps // 2
    period = -(-(frames + half) // 16) * 16
    omega = 2 * np.pi * (np.arange(period // 2) + 0.5) / period
    angle = omega[:, None] * np.arange(frames)
    forward = np.concatenate([np.cos(angle), np.sin(angle)], axis=0)
    lag_angle = omega[:, None] * (np.arange(taps) - half)
    tap_wave = np.concatenate([np.cos(lag_angle), np.sin(lag_angle)], axis=0)
    tap_wave = np.pad(tap_wave, ((0, 0), (0, 1)))
    lag_wave = np.concatenate([np.cos(lag_angle), -np.sin(lag_angle)], axis=0).T * (2 / period)
    lag_wave = np.pad(lag_wave, ((0, 1), (0, 0)))
    tap_high = tap_wave.astype(ml_dtypes.bfloat16)
    tap_low = (tap_wave - tap_high.astype(np.float64)).astype(ml_dtypes.bfloat16)
    return (
        split_const(forward),
        split_const(forward.T * (2 / period)),
        np.stack([tap_high, tap_low]),
        split_const(lag_wave),
        period,
    )


def terms(values):
    high = values.astype(BF16)
    low = (values - high.astype(F32)).astype(BF16)
    return jnp.concatenate([high, low, high], axis=0)


def wide_dot(const_terms, values):
    return jnp.dot(const_terms, terms(values), preferred_element_type=F32)


def down_lanes(row, width):
    frames = row.shape[1]
    square = jnp.broadcast_to(row, (frames, frames)).T
    return jnp.concatenate([square] * (width // frames), axis=1)


def across_lanes(first, second):
    frames = first.shape[0]
    lane = lax.broadcasted_iota(jnp.int32, (frames, frames), 1)
    square = jnp.where(lane == 0, first, jnp.where(lane == 1, second, 0.0))
    return square.T[0:8]


def row_stats(stat_refs, part_width):
    total = part_width * len(stat_refs)
    sums = [ref[0, 0:1, :] for ref in stat_refs]
    squares = [ref[0, 1:2, :] for ref in stat_refs]
    mean = sum(sums) / total
    spread = sum(squares)
    for part_sum in sums:
        shift = part_sum / part_width - mean
        spread = spread + part_width * (shift * shift)
    return mean, lax.rsqrt(spread / total + 1e-05)


def stats_kernel(order_ref, x_ref, dy_ref, dy_out, stat_out):
    dy_out[...] = dy_ref[...]
    values = x_ref[0].astype(F32)
    part_width = values.shape[1]
    part_sum = jnp.sum(values, axis=1, keepdims=True)
    centre = values - part_sum / part_width
    stat_out[0] = across_lanes(part_sum, jnp.sum(centre * centre, axis=1, keepdims=True))


def tap_kernel(wave_ref, tap_ref, out_ref):
    taps = tap_ref[0]
    out_ref[0] = jnp.dot(wave_ref[0], taps, preferred_element_type=F32) + jnp.dot(
        wave_ref[1], taps, preferred_element_type=F32
    )


def normed_of(x_ref, stat_refs):
    values = x_ref[0].astype(F32)
    width = values.shape[1]
    mean, inv_std = row_stats(stat_refs, width)
    return (values - down_lanes(mean, width)) * down_lanes(inv_std, width)


def front_kernel(parts, order_ref, lang_ref, x_ref, *refs):
    stat_refs, (gain_ref, tap_ref, fwd_ref, inv_ref, hid_out, conv_out, wave_out) = (
        refs[:parts],
        refs[parts:],
    )
    scaled = normed_of(x_ref, stat_refs) * gain_ref[0].astype(F32)
    wave = wide_dot(fwd_ref[...], scaled)
    count = wave.shape[0] // 2
    a, b = wave[:count], wave[count:]
    kc, ks = tap_ref[0, :count], tap_ref[0, count:]
    conv = wide_dot(inv_ref[...], jnp.concatenate([a * kc + b * ks, b * kc - a * ks], axis=0))
    hid_out[0] = (conv * jax.nn.sigmoid(conv)).astype(BF16)
    conv_out[0] = conv
    wave_out[0] = wave


def back_kernel(parts, cap, order_ref, lang_ref, mine_ref, x_ref, *refs):
    stat_refs = refs[:parts]
    (
        gain_ref,
        tap_ref,
        fwd_ref,
        inv_ref,
        lag_ref,
        own_ref,
        recv_ref,
        conv_ref,
        wave_ref,
        grad_out,
        sum_out,
        small_out,
        cross_acc,
        gain_acc,
    ) = refs[parts:]
    step = pl.program_id(0)

    @pl.when(step % cap == 0)
    def _():
        cross_acc[...] = jnp.zeros_like(cross_acc)
        gain_acc[...] = jnp.zeros_like(gain_acc)

    normed = normed_of(x_ref, stat_refs)
    frames, width = normed.shape
    conv = conv_ref[0]
    gate = jax.nn.sigmoid(conv)
    hid_grad = jnp.where(mine_ref[step // cap] > 0, own_ref[0], recv_ref[0]).astype(F32)
    conv_grad = hid_grad * gate * (1.0 + conv * (1.0 - gate))
    grad_wave = wide_dot(fwd_ref[...], conv_grad)
    count = grad_wave.shape[0] // 2
    ga, gb = grad_wave[:count], grad_wave[count:]
    a, b = wave_ref[0, :count], wave_ref[0, count:]
    kc, ks = tap_ref[0, :count], tap_ref[0, count:]
    cross_acc[:count] += ga * a + gb * b
    cross_acc[count:] += gb * a - ga * b
    scaled_grad = wide_dot(
        inv_ref[...], jnp.concatenate([ga * kc - gb * ks, ga * ks + gb * kc], axis=0)
    )
    gain_acc[...] += jnp.sum((scaled_grad * normed).reshape(frames // 8, 8, width), axis=0)
    norm_grad = scaled_grad * gain_ref[0].astype(F32)
    grad_out[0] = norm_grad
    sum_out[0] = across_lanes(
        jnp.sum(norm_grad, axis=1, keepdims=True),
        jnp.sum(norm_grad * normed, axis=1, keepdims=True),
    )

    @pl.when(step % cap == cap - 1)
    def _():
        tap_rows = wide_dot(lag_ref[...], cross_acc[...])
        gain_row = jnp.sum(gain_acc[...], axis=0, keepdims=True)
        row = lax.broadcasted_iota(jnp.int32, tap_rows.shape, 0)
        small_out[0] = jnp.where(row == tap_rows.shape[0] - 1, gain_row, tap_rows)


def final_kernel(parts, order_ref, x_ref, dy_ref, grad_ref, *refs):
    stat_refs, sum_refs, out_ref = refs[:parts], refs[parts : 2 * parts], refs[2 * parts]
    values = x_ref[0].astype(F32)
    width = values.shape[1]
    mean, inv_std = row_stats(stat_refs, width)
    spread = down_lanes(inv_std, width)
    normed = (values - down_lanes(mean, width)) * spread
    total = width * parts
    grad_mean = sum(ref[0, 0:1, :] for ref in sum_refs) / total
    cross_mean = sum(ref[0, 1:2, :] for ref in sum_refs) / total
    branch = spread * (
        grad_ref[0] - down_lanes(grad_mean, width) - normed * down_lanes(cross_mean, width)
    )
    out_ref[0] = (dy_ref[0].astype(F32) + branch).astype(BF16)


def hid_grad_kernel(parts, pick_ref, *refs):
    dy_refs = refs[:parts]
    w_refs, (out_ref, w_buf, sems) = refs[parts:-3], refs[-3:]
    step = pl.program_id(0)
    groups, _, width = w_buf.shape[0], w_buf.shape[1], dy_refs[0].shape[2]
    me = pick_ref[groups]

    def fetch(group, source):
        return pltpu.make_async_copy(source, w_buf.at[group], sems.at[group])

    @pl.when(step == 0)
    def _():
        for group in range(groups):
            for index, source in enumerate(w_refs):

                @pl.when(pick_ref[group] == index)
                def _():
                    fetch(group, source).start()

    @pl.when(pick_ref[step] >= 0)
    def _():
        fetch(step, w_refs[0]).wait()
        total = None
        for part, dy_ref in enumerate(dy_refs):
            columns = pl.ds(pl.multiple_of((me ^ part) * width, 128), width)
            term = lax.dot_general(
                dy_ref[0],
                w_buf[step, :, columns],
                (((1,), (1,)), ((), ())),
                preferred_element_type=F32,
            )
            total = term if total is None else total + term
        out_ref[0] = total.astype(BF16)


def w_grad_kernel(parts, scale, adds, pick_ref, *refs):
    hid_refs, dy_refs = refs[:2], refs[2 : 2 + 2 * parts]
    add_refs = refs[2 + 2 * parts : 2 + 2 * parts + adds]
    out_ref, hid_buf, dy_buf, sems = refs[2 + 2 * parts + adds :]
    width = hid_buf.shape[2]
    me = pick_ref[2]

    def copy_of(side, part):
        group = jnp.maximum(pick_ref[side], 0)
        if part == parts:
            source, held = hid_refs[side], hid_buf.at[side]
        else:
            source, held = dy_refs[side * parts + part], dy_buf.at[side, part]
        return pltpu.make_async_copy(source.at[group], held, sems.at[side, part])

    for side in range(2):

        @pl.when(pick_ref[side] >= 0)
        def _():
            for part in (parts, *range(parts)):
                copy_of(side, part).start()

    for side in range(2):

        @pl.when(pick_ref[side] >= 0)
        def _():
            copy_of(side, parts).wait()

    for part in range(parts):
        columns = pl.ds(pl.multiple_of((me ^ part) * width, 128), width)

        def product(side):
            return lax.dot_general(
                hid_buf[side],
                dy_buf[side, part],
                (((0,), (0,)), ((), ())),
                preferred_element_type=F32,
            )

        def put(total):
            for add_ref in add_refs:
                total = total + add_ref[:, columns].astype(F32)
            out_ref[:, columns] = (total * scale).astype(BF16)

        for side in range(2):

            @pl.when(pick_ref[side] >= 0)
            def _():
                copy_of(side, part).wait()

        first, second = pick_ref[0] >= 0, pick_ref[1] >= 0

        @pl.when(first & second)
        def _():
            put(product(0) + product(1))

        @pl.when(first & jnp.logical_not(second))
        def _():
            put(product(0))

        @pl.when(jnp.logical_not(first) & second)
        def _():
            put(product(1))

        @pl.when(jnp.logical_not(first | second) & (pick_ref[3] > 0))
        def _():
            put(jnp.zeros((out_ref.shape[0], width), F32))


def moved_weights(feats, cotan, lang, w_out, gain, kernel):
    segs, frames, width = feats.shape
    owners = lax.axis_size("expert")
    parts = lax.axis_size("fsdp")
    line = owners // 2
    cap = max(1, 2 * segs // owners)
    groups = segs // cap
    taps = kernel.shape[1]
    rows, total_width = w_out.shape[1:]
    owner = lax.axis_index("expert")
    place, side = owner // 2, owner % 2
    me = lax.axis_index("fsdp")
    forward, inverse, tap_wave, lag_wave, period = wave_tables(frames, taps)
    grad_scale = float(segs * frames) ** (-0.5)

    def pair_swap(value):
        return lax.ppermute(value, "expert", [(i, i ^ 1) for i in range(owners)])

    def along(value, places, step):
        pairs = [(2 * p + s, 2 * (p + step) + s) for p in places for s in range(2)]
        return lax.ppermute(value, "expert", pairs)

    def fsdp_swap(value, bit):
        return lax.ppermute(value, "fsdp", [(i, i ^ bit) for i in range(parts)])

    def fsdp_all(value):
        found = {0: value}
        bit = parts // 2
        while bit:
            found.update({key ^ bit: fsdp_swap(one, bit) for key, one in list(found.items())})
            bit //= 2
        return [found[key] for key in range(parts)]

    def params(**kwargs):
        return pltpu.CompilerParams(vmem_limit_bytes=48 * MIB, **kwargs)

    position = jnp.arange(segs, dtype=jnp.int32)
    before = (lang[None, :] < lang[:, None]) | (
        (lang[None, :] == lang[:, None]) & (position[None, :] < position[:, None])
    )
    rank = jnp.sum(before.astype(jnp.int32), axis=1)
    placed = rank[None, :] == position[:, None]
    order = jnp.sum(jnp.where(placed, position[None, :], 0), axis=1)
    lang_sorted = jnp.sum(jnp.where(placed, lang[None, :], 0), axis=1)
    group_lang = lang_sorted.reshape(groups, cap)[:, 0]
    pair_lang = pair_swap(group_lang)

    tap_rows = jnp.concatenate([kernel[0], gain], axis=0)
    all_rows = lax.all_gather(tap_rows, "expert", axis=0)
    all_gain = all_rows[:, taps:]

    seg_block = (1, frames, width)
    row_block = (1, 8, frames)
    by_order = pl.BlockSpec(seg_block, lambda i, o, *_: (o[i], 0, 0))
    in_turn = pl.BlockSpec(seg_block, lambda i, *_: (i, 0, 0))
    row_turn = pl.BlockSpec(row_block, lambda i, *_: (i, 0, 0))

    def whole(array):
        return pl.BlockSpec(array.shape, lambda *_: (0,) * array.ndim)

    def like(shape, dtype):
        return jax.ShapeDtypeStruct(shape, dtype)

    seg_bytes = segs * frames * width

    def cost(flops, moved):
        return pl.CostEstimate(flops=int(flops), bytes_accessed=int(moved), transcendentals=0)

    dy_sorted, stats = pl.pallas_call(
        stats_kernel,
        grid_spec=pltpu.PrefetchScalarGridSpec(
            num_scalar_prefetch=1,
            grid=(segs,),
            in_specs=[by_order, by_order],
            out_specs=[in_turn, row_turn],
        ),
        out_shape=[like(feats.shape, BF16), like((segs, 8, frames), F32)],
        compiler_params=params(),
        cost_estimate=cost(5 * seg_bytes, 6 * seg_bytes),
        name="frame_stats",
    )(order, feats, cotan)

    stat_parts = fsdp_all(stats)

    dy_pair = pair_swap(dy_sorted)
    group_shape = (groups, cap * frames, width)
    dy_parts = [part.reshape(group_shape) for part in fsdp_all(dy_sorted)]
    dy_pair_parts = [part.reshape(group_shape) for part in fsdp_all(dy_pair)]

    w_own = w_out[0]
    from_left, from_right = [w_own], [w_own]
    for step in range(1, line):
        from_left.append(along(from_left[-1], range(step - 1, line - 1), 1))
        from_right.append(along(from_right[-1], range(1, line - step + 1), -1))
    w_held = [w_own] + from_left[1:] + from_right[1:]

    tap_table = pl.pallas_call(
        tap_kernel,
        grid=(owners,),
        in_specs=[whole(tap_wave), pl.BlockSpec((1, taps + 1, width), lambda i: (i, 0, 0))],
        out_specs=pl.BlockSpec((1, period, width), lambda i: (i, 0, 0)),
        out_shape=like((owners, period, width), F32),
        compiler_params=params(),
        cost_estimate=cost(4 * owners * period * taps * width, 4 * owners * period * width),
        name="tap_waves",
    )(jnp.asarray(tap_wave), all_rows)

    gain_spec = pl.BlockSpec((1, 1, width), lambda i, o, l, *_: (l[i], 0, 0))
    tap_spec = pl.BlockSpec((1, period, width), lambda i, o, l, *_: (l[i], 0, 0))
    wave_turn = pl.BlockSpec((1, period, width), lambda i, *_: (i, 0, 0))
    forward_c, inverse_c, lag_c = jnp.asarray(forward), jnp.asarray(inverse), jnp.asarray(lag_wave)
    wave_flops = 12 * segs * period * frames * width

    hidden, conv, wave = pl.pallas_call(
        lambda *refs: front_kernel(parts, *refs),
        grid_spec=pltpu.PrefetchScalarGridSpec(
            num_scalar_prefetch=2,
            grid=(segs,),
            in_specs=[by_order]
            + [row_turn] * parts
            + [gain_spec, tap_spec, whole(forward), whole(inverse)],
            out_specs=[in_turn, in_turn, wave_turn],
        ),
        out_shape=[
            like(feats.shape, BF16),
            like(feats.shape, F32),
            like((segs, period, width), F32),
        ],
        compiler_params=params(),
        cost_estimate=cost(wave_flops, 14 * seg_bytes),
        name="front",
    )(order, lang_sorted, feats, *stat_parts, all_gain, tap_table, forward_c, inverse_c)

    hidden = hidden.reshape(group_shape)
    hidden_pair = pair_swap(hidden)

    def picks(langs):
        far = langs // 2 - place
        index = jnp.where(far <= 0, -far, line - 1 + far)
        return jnp.where(langs % 2 == side, index, -1)

    any_spec = pl.BlockSpec(memory_space=pl.ANY)

    def hid_grad_of(langs, dys):
        pick = jnp.concatenate([picks(langs), me.reshape(1)]).astype(jnp.int32)
        return pl.pallas_call(
            lambda *refs: hid_grad_kernel(parts, *refs),
            grid_spec=pltpu.PrefetchScalarGridSpec(
                num_scalar_prefetch=1,
                grid=(groups,),
                in_specs=[pl.BlockSpec((1,) + group_shape[1:], lambda i, *_: (i, 0, 0))] * parts
                + [any_spec] * len(w_held),
                out_specs=pl.BlockSpec((1,) + group_shape[1:], lambda i, *_: (i, 0, 0)),
                scratch_shapes=[
                    pltpu.VMEM((groups, rows, total_width), BF16),
                    pltpu.SemaphoreType.DMA((groups,)),
                ],
            ),
            out_shape=like(group_shape, BF16),
            compiler_params=params(),
            cost_estimate=cost(2 * seg_bytes * total_width, 2 * seg_bytes * (parts + 3)),
            name="hid_grad",
        )(pick, *dys, *w_held)

    hid_grad_pair = pair_swap(hid_grad_of(pair_lang, dy_pair_parts))
    hid_grad_own = hid_grad_of(group_lang, dy_parts)

    def w_grad_of(target, adds, scale):
        language = 2 * target + side
        valid = (target >= 0) & (target < line)
        slot = jnp.arange(groups, dtype=jnp.int32)

        def where_is(langs):
            return jnp.max(jnp.where((langs == language) & valid, slot, -1))

        pick = jnp.stack(
            [where_is(group_lang), where_is(pair_lang), me, valid.astype(jnp.int32)]
        ).astype(jnp.int32)
        return pl.pallas_call(
            lambda *refs: w_grad_kernel(parts, scale, len(adds), *refs),
            grid_spec=pltpu.PrefetchScalarGridSpec(
                num_scalar_prefetch=1,
                grid=(1,),
                in_specs=[any_spec] * (2 + 2 * parts) + [whole(w_own)] * len(adds),
                out_specs=whole(w_own),
                scratch_shapes=[
                    pltpu.VMEM((2,) + group_shape[1:], BF16),
                    pltpu.VMEM((2, parts) + group_shape[1:], BF16),
                    pltpu.SemaphoreType.DMA((2, parts + 1)),
                ],
            ),
            out_shape=like(w_own.shape, BF16),
            compiler_params=params(),
            cost_estimate=cost(4 * cap * frames * rows * total_width, 6 * rows * total_width),
            name="w_grad",
        )(pick, hidden, hidden_pair, *dy_parts, *dy_pair_parts, *adds)

    right, left = (), ()
    for step in range(1, line):
        send_right = w_grad_of(place + line - step, right, 1.0)
        send_left = w_grad_of(place - line + step, left, 1.0)
        right = (along(send_right, range(0, step), 1),)
        left = (along(send_left, range(line - step, line), -1),)
    w_grad = w_grad_of(place, right + left, grad_scale)

    mine = (group_lang % 2 == side).astype(jnp.int32)
    small_spec = pl.BlockSpec((1, taps + 1, width), lambda i, *_: (i // cap, 0, 0))
    norm_grad, sums, small = pl.pallas_call(
        lambda *refs: back_kernel(parts, cap, *refs),
        grid_spec=pltpu.PrefetchScalarGridSpec(
            num_scalar_prefetch=3,
            grid=(segs,),
            in_specs=[by_order]
            + [row_turn] * parts
            + [gain_spec, tap_spec, whole(forward), whole(inverse), whole(lag_wave)]
            + [in_turn, in_turn, in_turn, wave_turn],
            out_specs=[in_turn, row_turn, small_spec],
            scratch_shapes=[pltpu.VMEM((period, width), F32), pltpu.VMEM((8, width), F32)],
        ),
        out_shape=[
            like(feats.shape, F32),
            like((segs, 8, frames), F32),
            like((groups, taps + 1, width), F32),
        ],
        compiler_params=params(),
        cost_estimate=cost(wave_flops, 20 * seg_bytes),
        name="back",
    )(
        order,
        lang_sorted,
        mine,
        feats,
        *stat_parts,
        all_gain,
        tap_table,
        forward_c,
        inverse_c,
        lag_c,
        hid_grad_own.reshape(feats.shape),
        hid_grad_pair.reshape(feats.shape),
        conv,
        wave,
    )
    sum_parts = fsdp_all(sums)
    feat_grad = pl.pallas_call(
        lambda *refs: final_kernel(parts, *refs),
        grid_spec=pltpu.PrefetchScalarGridSpec(
            num_scalar_prefetch=1,
            grid=(segs,),
            in_specs=[by_order, in_turn, in_turn] + [row_turn] * (2 * parts),
            out_specs=by_order,
        ),
        out_shape=like(feats.shape, BF16),
        compiler_params=params(),
        cost_estimate=cost(10 * seg_bytes, 10 * seg_bytes),
        name="input_grad",
    )(order, feats, dy_sorted, norm_grad, *stat_parts, *sum_parts)

    slots = jnp.arange(owners, dtype=jnp.int32)[:, None] == group_lang[None, :]
    spread = jnp.sum(jnp.where(slots[:, :, None, None], small[None], 0.0), axis=1)
    arrived = lax.all_to_all(spread, "expert", split_axis=0, concat_axis=0, tiled=True)
    small_sum = jnp.sum(arrived, axis=0) * grad_scale
    return (feat_grad, w_grad[None], small_sum[taps:], small_sum[None, :taps])


def per_device(feats, cotan, lang, w_out, gain, kernel):
    segs, frames, width = feats.shape
    owners = lax.axis_size("expert")
    parts = lax.axis_size("fsdp")
    weights_moved = 2 * (owners // 2 - 1) * math.prod(w_out.shape)
    frames_moved = 3 * 2 * math.prod(feats.shape)
    fits = owners % 2 == 0 and parts & (parts - 1) == 0 and frames % 128 == 0 and width % frames == 0
    if fits and weights_moved < frames_moved:
        return moved_weights(feats, cotan, lang, w_out, gain, kernel)
    return routed_frames(feats, cotan, lang, w_out, gain, kernel)


def solution(mesh):
    in_specs = (
        P("expert", None, "fsdp"),
        P("expert", None, "fsdp"),
        P("expert"),
        P("expert", "fsdp", None),
        P("expert", "fsdp"),
        P("expert", None, "fsdp"),
    )
    out_specs = (
        P("expert", None, "fsdp"),
        P("expert", "fsdp", None),
        P("expert", "fsdp"),
        P("expert", None, "fsdp"),
    )
    return jax.shard_map(
        per_device, mesh=mesh, in_specs=in_specs, out_specs=out_specs, check_vma=False
    )
```

```python
import math

import jax
import jax.numpy as jnp
import ml_dtypes
import numpy as np
from jax import lax
from jax.experimental import pallas as pl
from jax.experimental.pallas import tpu as pltpu
from jax.sharding import PartitionSpec as P

BF16 = jnp.bfloat16
F32 = jnp.float32
VMEM_BYTES = 60 * 1024 * 1024
WEIGHT = {"front": 30, "frame_stats": 30, "tap_waves": 30, "w_grad": 30}

def normalize(values, feature_total):
    value_sum = lax.psum(jnp.sum(values, axis=-1), "fsdp")
    centre = values - (value_sum / feature_total)[..., None]
    square_sum = lax.psum(jnp.sum(centre * centre, axis=-1), "fsdp")
    row_var = square_sum / feature_total
    inv_std = lax.rsqrt(row_var + 1e-05)[..., None]
    return (centre * inv_std, inv_std)


def forward_part(inputs, norm_gain, conv_taps, feature_total):
    normed, inv_std = normalize(inputs.astype(jnp.float32), feature_total)
    scaled = normed * norm_gain
    tap_count = conv_taps.shape[0]
    half_width = tap_count // 2
    frames = inputs.shape[1]
    padded = jnp.pad(scaled, ((0, 0), (half_width, half_width), (0, 0)))
    conv_out = jnp.zeros_like(scaled)
    for offset in range(tap_count):
        conv_out = conv_out + conv_taps[offset] * padded[:, offset : offset + frames]
    gate_sig = jax.nn.sigmoid(conv_out)
    hidden = (conv_out * gate_sig).astype(jnp.bfloat16)
    return (normed, inv_std, padded, conv_out, gate_sig, hidden)


def back_split(
    hid_grad,
    grads_in,
    normed,
    inv_std,
    padded,
    conv_out,
    gate_sig,
    norm_gain,
    conv_taps,
    feature_total,
):
    tap_count = conv_taps.shape[0]
    half_width = tap_count // 2
    frames = normed.shape[1]
    conv_grad = hid_grad * gate_sig * (1.0 + conv_out * (1.0 - gate_sig))
    grad_padded = jnp.pad(conv_grad, ((0, 0), (half_width, half_width), (0, 0)))
    scaled_grad = jnp.zeros_like(conv_grad)
    tap_grads = []
    for offset in range(tap_count):
        first_row = 2 * half_width - offset
        scaled_grad = (
            scaled_grad + conv_taps[offset] * grad_padded[:, first_row : first_row + frames]
        )
        tap_grads.append(jnp.sum(conv_grad * padded[:, offset : offset + frames], axis=(0, 1)))
    gain_grad = jnp.sum(scaled_grad * normed, axis=(0, 1))
    norm_grad = scaled_grad * norm_gain
    grad_total, cross_total = lax.psum(
        (jnp.sum(norm_grad, axis=-1), jnp.sum(norm_grad * normed, axis=-1)), "fsdp"
    )
    branch = inv_std * (
        norm_grad
        - (grad_total / feature_total)[..., None]
        - normed * (cross_total / feature_total)[..., None]
    )
    input_grad = (grads_in.astype(jnp.float32) + branch).astype(jnp.bfloat16)
    return (input_grad, gain_grad, jnp.stack(tap_grads))


def arrival_map(recv_occupied, seg_count):
    flat_occupied = recv_occupied.reshape(-1)
    order_pos = jnp.cumsum(flat_occupied) - 1
    position = jnp.arange(seg_count, dtype=jnp.int32)
    return ((order_pos[None, :] == position[:, None]) & (flat_occupied[None, :] > 0)).astype(
        jnp.bfloat16
    )


def compact_rows(compact_map, received, row_shape):
    flat = received.reshape(compact_map.shape[1], -1)
    return (
        jnp.dot(compact_map, flat, preferred_element_type=jnp.float32)
        .astype(jnp.bfloat16)
        .reshape(row_shape)
    )


def routed_frames(feats, cotan, lang, w_out, gain, kernel):
    seg_count, frames, part_width = feats.shape
    owners = lax.axis_size("expert")
    feature_total = part_width * lax.axis_size("fsdp")
    capacity = max(1, 2 * seg_count // owners)
    slot_count = owners * capacity
    position = jnp.arange(seg_count, dtype=jnp.int32)
    earlier_same = (lang[:, None] == lang[None, :]) & (position[:, None] < position[None, :])
    slot_rank = jnp.sum(earlier_same.astype(jnp.int32), axis=0)
    slot_of = lang * capacity + slot_rank
    routing = jnp.arange(slot_count, dtype=jnp.int32)[:, None] == slot_of[None, :]
    routing_b = routing.astype(jnp.bfloat16)
    send_x = (
        jnp.dot(routing_b, feats.reshape(seg_count, -1), preferred_element_type=jnp.float32)
        .astype(jnp.bfloat16)
        .reshape(owners, capacity, -1)
    )
    send_dy = (
        jnp.dot(routing_b, cotan.reshape(seg_count, -1), preferred_element_type=jnp.float32)
        .astype(jnp.bfloat16)
        .reshape(owners, capacity, -1)
    )
    occupied = jnp.sum(routing.astype(jnp.int32), axis=1).reshape(owners, capacity)
    norm_gain = gain[0].astype(jnp.float32)
    conv_taps = kernel[0].astype(jnp.float32)
    row_shape = (seg_count, frames, part_width)
    recv_x, recv_dy, recv_occupied = (
        lax.all_to_all(send_x, "expert", split_axis=0, concat_axis=0, tiled=True),
        lax.all_to_all(send_dy, "expert", split_axis=0, concat_axis=0, tiled=True),
        lax.all_to_all(occupied, "expert", split_axis=0, concat_axis=0, tiled=True),
    )
    compact_map = arrival_map(recv_occupied, seg_count)
    own_x = compact_rows(compact_map, recv_x, row_shape)
    forward = forward_part(own_x, norm_gain, conv_taps, feature_total)
    own_dy = compact_rows(compact_map, recv_dy, row_shape)
    normed, inv_std, padded, conv_out, gate_sig, hidden = forward
    grad_scale = float(seg_count * frames) ** (-0.5)
    hidden_rows = hidden.reshape(-1, part_width)
    w_rows = w_out[0]
    shard_part = lax.all_gather(own_dy.reshape(-1, part_width), "fsdp", axis=1, tiled=True)
    hid_sum = jnp.dot(shard_part, w_rows.T, preferred_element_type=jnp.float32)
    w_block = jnp.dot(hidden_rows.T, shard_part, preferred_element_type=jnp.float32) * grad_scale
    w_sum = w_block
    hid_sum, w_sum = (hid_sum, w_sum)
    hid_grad = hid_sum.reshape(row_shape)
    input_grad, gain_grad, tap_grad = back_split(
        hid_grad,
        own_dy,
        normed,
        inv_std,
        padded,
        conv_out,
        gate_sig,
        norm_gain,
        conv_taps,
        feature_total,
    )
    back_slots = jnp.dot(
        compact_map.T, input_grad.reshape(seg_count, -1), preferred_element_type=jnp.float32
    ).astype(jnp.bfloat16)
    home_slots = lax.all_to_all(
        back_slots.reshape(owners, capacity, -1), "expert", split_axis=0, concat_axis=0, tiled=True
    )
    feat_grad = (
        jnp.dot(routing_b.T, home_slots.reshape(slot_count, -1), preferred_element_type=jnp.float32)
        .astype(jnp.bfloat16)
        .reshape(feats.shape)
    )
    return (
        feat_grad,
        w_sum.astype(jnp.bfloat16)[None],
        (gain_grad * grad_scale)[None],
        (tap_grad * grad_scale)[None],
    )


def split_const(matrix):
    high = matrix.astype(ml_dtypes.bfloat16)
    low = (matrix - high.astype(np.float64)).astype(ml_dtypes.bfloat16)
    return np.concatenate([high, high, low], axis=1)


def wave_tables(frames, taps):
    half = taps // 2
    period = -(-(frames + half) // 16) * 16
    omega = 2 * np.pi * (np.arange(period // 2) + 0.5) / period
    angle = omega[:, None] * np.arange(frames)
    forward = np.concatenate([np.cos(angle), np.sin(angle)], axis=0)
    lag_angle = omega[:, None] * (np.arange(taps) - half)
    tap_wave = np.concatenate([np.cos(lag_angle), np.sin(lag_angle)], axis=0)
    tap_wave = np.pad(tap_wave, ((0, 0), (0, 1)))
    lag_wave = np.concatenate([np.cos(lag_angle), -np.sin(lag_angle)], axis=0).T * (2 / period)
    lag_wave = np.pad(lag_wave, ((0, 1), (0, 0)))
    tap_high = tap_wave.astype(ml_dtypes.bfloat16)
    tap_low = (tap_wave - tap_high.astype(np.float64)).astype(ml_dtypes.bfloat16)
    return (
        split_const(forward),
        split_const(forward.T * (2 / period)),
        np.stack([tap_high, tap_low]),
        split_const(lag_wave),
        period,
    )


def wide_dot(const_terms, values):
    high = values.astype(BF16)
    low = (values - high.astype(F32)).astype(BF16)
    stacked = jnp.concatenate([high, low, high], axis=0)
    return jnp.dot(const_terms, stacked, preferred_element_type=F32)


def down_lanes(row, width):
    frames = row.shape[1]
    square = jnp.broadcast_to(row, (frames, frames)).T
    return jnp.concatenate([square] * (width // frames), axis=1)


def across_lanes(first, second):
    frames = first.shape[0]
    lane = lax.broadcasted_iota(jnp.int32, (frames, frames), 1)
    square = jnp.where(lane == 0, first, jnp.where(lane == 1, second, 0.0))
    return square.T[0:8]


def side_by_side(pieces):
    return jnp.concatenate(pieces, axis=1) if len(pieces) > 1 else pieces[0]


def row_stats(stat_refs, part_width):
    total = part_width * len(stat_refs)
    sums = [ref[0, 0:1, :] for ref in stat_refs]
    squares = [ref[0, 1:2, :] for ref in stat_refs]
    mean = sum(sums) / total
    spread = sum(squares)
    for part_sum in sums:
        shift = part_sum / part_width - mean
        spread = spread + part_width * (shift * shift)
    return mean, lax.rsqrt(spread / total + 1e-05)


def stats_kernel(x_ref, stat_out):
    for one in range(x_ref.shape[0]):
        values = x_ref[one].astype(F32)
        part_width = values.shape[1]
        part_sum = jnp.sum(values, axis=1, keepdims=True)
        centre = values - part_sum / part_width
        stat_out[one] = across_lanes(part_sum, jnp.sum(centre * centre, axis=1, keepdims=True))


def tap_kernel(wave_ref, *refs):
    tap_refs, out_ref = refs[:-1], refs[-1]
    period, count = wave_ref.shape[1:]
    at = 0
    for tap_ref in tap_refs:
        for one in range(tap_ref.shape[0]):
            taps = tap_ref[one, :count]
            out_ref[at, :period] = jnp.dot(
                wave_ref[0], taps, preferred_element_type=F32
            ) + jnp.dot(wave_ref[1], taps, preferred_element_type=F32)
            gain = taps.astype(F32)[taps.shape[0] - 1 :]
            out_ref[at, period:] = jnp.broadcast_to(gain, (8, gain.shape[1]))
            at += 1


def normed_of(x_ref, rows):
    values = x_ref[0].astype(F32)
    width = values.shape[1]
    spread = down_lanes(rows[1:2], width)
    return (values - down_lanes(rows[0:1], width)) * spread, spread


def front_kernel(cap, parts, own_ref, *refs):
    refs = list(refs)
    x_refs = [refs.pop(0) for _ in range(cap)]
    stat_refs = [[refs.pop(0) for _ in range(cap)] for _ in range(parts)]
    tap_ref, fwd_ref, inv_ref, *hid_outs, conv_out, wave_out, row_out = refs
    width = x_refs[0].shape[2]
    period = wave_out.shape[1]
    gain = tap_ref[0, period : period + 1]
    scaled = []
    for one in range(cap):
        mean, inv_std = row_stats([ref[one] for ref in stat_refs], width)
        row = lax.broadcasted_iota(jnp.int32, row_out.shape[1:], 0)
        rows = jnp.where(row == 0, mean, jnp.where(row == 1, inv_std, 0.0))
        row_out[one] = rows
        scaled.append(normed_of(x_refs[one], rows)[0] * gain)
    wave = wide_dot(fwd_ref[...], side_by_side(scaled))
    count = wave.shape[0] // 2
    a, b = wave[:count], wave[count:]
    kc = side_by_side([tap_ref[0, :count]] * cap)
    ks = side_by_side([tap_ref[0, count : 2 * count]] * cap)
    conv = wide_dot(inv_ref[...], jnp.concatenate([a * kc + b * ks, b * kc - a * ks], axis=0))
    hidden = (conv * jax.nn.sigmoid(conv)).astype(BF16)
    frames = conv.shape[0]
    for one in range(cap):
        at = slice(one * width, (one + 1) * width)
        conv_out[one] = conv[:, at]
        wave_out[one] = wave[:, at]
        first = one * width
        for hid_out in hid_outs:
            cut = hid_out.shape[2]
            hid_out[0, one * frames : (one + 1) * frames] = hidden[:, first : first + cut]
            first += cut


def back_kernel(cap, own_ref, *refs):
    x_refs = refs[:cap]
    (
        row_ref,
        tap_ref,
        fwd_ref,
        inv_ref,
        lag_ref,
        own_grad_ref,
        recv_ref,
        conv_ref,
        wave_ref,
        grad_out,
        sum_out,
        small_out,
    ) = refs[cap:]
    segs = conv_ref.shape[0] * pl.num_programs(0)
    period = wave_ref.shape[1]
    mine = (own_ref[segs + pl.program_id(0) * cap] & 1) == (own_ref[2 * segs] & 1)
    gain = tap_ref[0, period : period + 1]
    frames, width = x_refs[0].shape[1:]
    normed = [normed_of(x_refs[one], row_ref[one])[0] for one in range(cap)]
    hid_grad = jnp.where(mine, own_grad_ref[0], recv_ref[0]).astype(F32)
    hid_grad = side_by_side([hid_grad[one * frames : (one + 1) * frames] for one in range(cap)])
    conv = side_by_side([conv_ref[one] for one in range(cap)])
    gate = jax.nn.sigmoid(conv)
    conv_grad = hid_grad * gate * (1.0 + conv * (1.0 - gate))
    grad_wave = wide_dot(fwd_ref[...], conv_grad)
    count = grad_wave.shape[0] // 2
    ga, gb = grad_wave[:count], grad_wave[count:]
    wave = side_by_side([wave_ref[one] for one in range(cap)])
    a, b = wave[:count], wave[count:]
    kc = side_by_side([tap_ref[0, :count]] * cap)
    ks = side_by_side([tap_ref[0, count : 2 * count]] * cap)
    cross = jnp.concatenate([ga * a + gb * b, gb * a - ga * b], axis=0)
    cross = sum(cross[:, one * width : (one + 1) * width] for one in range(cap))
    scaled_grad = wide_dot(
        inv_ref[...], jnp.concatenate([ga * kc - gb * ks, ga * ks + gb * kc], axis=0)
    )
    gain_grad = None
    for one in range(cap):
        part = scaled_grad[:, one * width : (one + 1) * width]
        product = part * normed[one]
        gain_grad = product if gain_grad is None else gain_grad + product
        norm_grad = part * gain
        grad_out[one] = norm_grad
        sum_out[one] = across_lanes(
            jnp.sum(norm_grad, axis=1, keepdims=True),
            jnp.sum(norm_grad * normed[one], axis=1, keepdims=True),
        )
    tap_rows = wide_dot(lag_ref[...], cross)
    gain_row = jnp.sum(gain_grad, axis=0, keepdims=True)
    row = lax.broadcasted_iota(jnp.int32, tap_rows.shape, 0)
    small_out[0] = jnp.where(row == tap_rows.shape[0] - 1, gain_row, tap_rows)


def final_kernel(cap, chunks, order_ref, *refs):
    x_refs, dy_refs, grad_refs = refs[:cap], refs[cap : 2 * cap], refs[2 * cap : 2 * cap + chunks]
    row_ref, *sum_refs, out_ref, out_buf, sems = refs[2 * cap + chunks :]
    step, last = pl.program_id(0), pl.num_programs(0) - 1
    parts, width = len(sum_refs), x_refs[0].shape[2]
    slot = step % 2

    def put(slot, step, one):
        return pltpu.make_async_copy(
            out_buf.at[slot, one], out_ref.at[order_ref[step * cap + one]], sems.at[slot, one]
        )

    @pl.when(step >= 2)
    def _():
        for one in range(cap):
            put(slot, step - 2, one).wait()

    for one in range(cap):
        normed, spread = normed_of(x_refs[one], row_ref[one])
        total = width * parts
        grad_mean = sum(ref[one, 0:1, :] for ref in sum_refs) / total
        cross_mean = sum(ref[one, 1:2, :] for ref in sum_refs) / total
        grad = side_by_side([grad_ref[one] for grad_ref in grad_refs])
        branch = spread * (
            grad - down_lanes(grad_mean, width) - normed * down_lanes(cross_mean, width)
        )
        out_buf[slot, one] = (dy_refs[one][0].astype(F32) + branch).astype(BF16)
        put(slot, step, one).start()

    @pl.when(step == last)
    def _():
        for one in range(cap):
            put(slot, step, one).wait()

    @pl.when((step == last) & (step >= 1))
    def _():
        for one in range(cap):
            put(1 - slot, step - 1, one).wait()


def hid_grad_kernel(parts, cap, held, of_pair, own_ref, pair_ref, *refs):
    dy_refs, w_refs, out_refs = refs[:parts], refs[parts : parts + held], refs[parts + held : -4]
    dy_buf, w_buf, dy_sems, w_sems = refs[-4:]
    groups = w_buf.shape[0]
    segs = groups * cap
    frames, width = dy_refs[0].shape[1:]
    step = pl.program_id(0)
    owner, me = own_ref[2 * segs], own_ref[2 * segs + 1]
    table = pair_ref if of_pair else own_ref

    def held_index(group):
        language = table[segs + group * cap]
        index = ((owner >> 1) - (language >> 1)) & (held - 1)
        return jnp.where((language & 1) == (owner & 1), index, -1)

    def w_copy(group, source):
        return pltpu.make_async_copy(source, w_buf.at[group], w_sems.at[group])

    def dy_copy(group, part, one):
        return pltpu.make_async_copy(
            dy_refs[part].at[table[group * cap + one]],
            dy_buf.at[group, part, pl.ds(one * frames, frames)],
            dy_sems.at[group, part, one],
        )

    @pl.when(step == 0)
    def _():
        for group in range(groups):
            index = held_index(group)
            for at, source in enumerate(w_refs):

                @pl.when(index == at)
                def _():
                    w_copy(group, source).start()

            @pl.when(index >= 0)
            def _():
                for part in range(parts):
                    for one in range(cap):
                        dy_copy(group, part, one).start()

    @pl.when(held_index(step) >= 0)
    def _():
        w_copy(step, w_refs[0]).wait()
        total = None
        for part in range(parts):
            for one in range(cap):
                dy_copy(step, part, one).wait()
            columns = pl.ds(pl.multiple_of((me ^ part) * width, 128), width)
            term = lax.dot_general(
                dy_buf[step, part],
                w_buf[step, :, columns],
                (((1,), (1,)), ((), ())),
                preferred_element_type=F32,
            )
            total = term if total is None else total + term
        chunk = total.shape[1] // len(out_refs)
        for index, out_ref in enumerate(out_refs):
            out_ref[0] = total[:, index * chunk : (index + 1) * chunk].astype(BF16)


def w_grad_kernel(cap, segs, line, step, parts, places, scale, own_ref, pair_ref, *refs):
    refs = list(refs)

    def take(number):
        return [refs.pop(0) for _ in range(number)]

    hid_refs, dy_refs, add_refs = take(2), [take(parts), take(parts)], take(len(places))
    out_ref, hid_buf, dy_buf, add_buf, hid_sems, dy_sems, add_sems = refs
    width = dy_buf.shape[3]
    frames = dy_buf.shape[2] // cap
    owner, me = own_ref[2 * segs], own_ref[2 * segs + 1]
    language = 2 * (((owner >> 1) - step) & (line - 1)) + (owner & 1)
    found = []
    for table in (own_ref, pair_ref):
        group = jnp.int32(-1)
        for at in range(segs // cap):
            group = jnp.where(table[segs + at * cap] == language, at, group)
        found.append(group)

    def hid_copy(side):
        source = hid_refs[side].at[jnp.maximum(found[side], 0)]
        return pltpu.make_async_copy(source, hid_buf.at[side], hid_sems.at[side])

    def dy_copies(side, part):
        for one in range(cap):
            segment = (own_ref, pair_ref)[side][jnp.maximum(found[side], 0) * cap + one]
            yield pltpu.make_async_copy(
                dy_refs[side][part].at[segment],
                dy_buf.at[side, part, pl.ds(one * frames, frames)],
                dy_sems.at[side, part, one],
            )

    def add_copy(index):
        ref = add_refs[index]
        held = add_buf.at[:, pl.ds(places[index], ref.shape[1])]
        return pltpu.make_async_copy(ref, held, add_sems.at[index])

    for side in range(2):

        @pl.when(found[side] >= 0)
        def _():
            hid_copy(side).start()
            for part in range(parts):
                for copy in dy_copies(side, part):
                    copy.start()

    for index in range(len(places)):
        add_copy(index).start()
    for side in range(2):

        @pl.when(found[side] >= 0)
        def _():
            hid_copy(side).wait()

    first, second = found[0] >= 0, found[1] >= 0
    for index in range(len(places)):
        add_copy(index).wait()
    for part in range(parts):
        at = slice(part * width, (part + 1) * width)

        def product(side):
            return lax.dot_general(
                hid_buf[side],
                dy_buf[side, part],
                (((0,), (0,)), ((), ())),
                preferred_element_type=F32,
            )

        def put(value):
            if places:
                value = value + add_buf[:, at].astype(F32)
            if scale is None:
                out_ref[:, at] = value.astype(BF16)
            else:
                columns = pl.ds(pl.multiple_of((me ^ part) * width, 128), width)
                out_ref[:, columns] = (value * scale).astype(BF16)

        for side in range(2):

            @pl.when(found[side] >= 0)
            def _():
                for copy in dy_copies(side, part):
                    copy.wait()

        @pl.when(first & second)
        def _():
            put(product(0) + product(1))

        @pl.when(first & jnp.logical_not(second))
        def _():
            put(product(0))

        @pl.when(jnp.logical_not(first) & second)
        def _():
            put(product(1))

        @pl.when(jnp.logical_not(first | second))
        def _():
            put(jnp.zeros((out_ref.shape[0], width), F32))


def moved_weights(feats, cotan, lang, w_out, gain, kernel):
    segs, frames, width = feats.shape
    owners = lax.axis_size("expert")
    parts = lax.axis_size("fsdp")
    line = owners // 2
    cap = max(1, 2 * segs // owners)
    groups = segs // cap
    taps = kernel.shape[1]
    rows, total_width = w_out.shape[1:]
    owner = lax.axis_index("expert")
    me = lax.axis_index("fsdp")
    forward, inverse, tap_wave, lag_wave, period = wave_tables(frames, taps)
    grad_scale = float(segs * frames) ** (-0.5)
    chunk = 128
    chunks = width // chunk

    def pair_swap(value):
        return lax.ppermute(value, "expert", [(i, i ^ 1) for i in range(owners)])

    def along(value):
        return lax.ppermute(value, "expert", [(i, (i + 2) % owners) for i in range(owners)])

    def swap(value, bit):
        return lax.ppermute(value, "fsdp", [(i, i ^ bit) for i in range(parts)])

    def after(value, *others):
        return lax.optimization_barrier((value, *others))[0]

    def whole(array):
        return pl.BlockSpec(array.shape, lambda *_: (0,) * array.ndim)

    def like(shape, dtype):
        return jax.ShapeDtypeStruct(shape, dtype)

    order_of_calls = []

    def call(body, name, scalars, inputs, outputs, grid, scratch=(), flops=0, waits=()):
        if scalars:
            scalars = (after(scalars[0], *order_of_calls[-1:], *waits), *scalars[1:])
        arrays, in_specs = zip(*inputs)
        shapes, out_specs = zip(*outputs)
        moved = sum(math.prod(a.shape) * a.dtype.itemsize for a in (*arrays, *shapes))
        found = pl.pallas_call(
            body,
            grid_spec=pltpu.PrefetchScalarGridSpec(
                num_scalar_prefetch=len(scalars),
                grid=grid,
                in_specs=in_specs,
                out_specs=out_specs,
                scratch_shapes=scratch,
            ),
            out_shape=shapes,
            compiler_params=pltpu.CompilerParams(vmem_limit_bytes=VMEM_BYTES),
            cost_estimate=pl.CostEstimate(
                flops=int(flops * WEIGHT.get(name, 1)),
                bytes_accessed=int(moved * WEIGHT.get(name, 1)),
                transcendentals=0,
            ),
            name=name,
        )(*scalars, *arrays)
        order_of_calls.append(found[0])
        return list(found)

    any_spec = pl.BlockSpec(memory_space=pl.ANY)

    lang_row = jnp.pad(lang.astype(BF16), (0, width - segs))[None]
    tap_rows = jnp.concatenate([kernel[0], gain, lang_row], axis=0)
    tap_rows = jnp.pad(tap_rows, ((0, -tap_rows.shape[0] % 16), (0, 0)))[None]
    tap_rows = jnp.concatenate([tap_rows, pair_swap(tap_rows)], axis=0)
    tap_rows = [tap_rows] + [
        lax.ppermute(tap_rows, "expert", [(i, i ^ (2 * k)) for i in range(owners)])
        for k in range(1, line)
    ]
    per_step = 4 if segs % 4 == 0 else 1
    stats = call(
        stats_kernel,
        "frame_stats",
        (),
        [(feats, pl.BlockSpec((per_step, frames, width), lambda i: (i, 0, 0)))],
        [
            (
                like((segs, 8, frames), F32),
                pl.BlockSpec((per_step, 8, frames), lambda i: (i, 0, 0)),
            )
        ],
        (segs // per_step,),
    )[0]
    stat_parts = [stats] + [swap(stats, k) for k in range(1, parts)]

    def table_of(langs, *more):
        position = jnp.arange(segs, dtype=jnp.int32)
        before = (langs[None, :] < langs[:, None]) | (
            (langs[None, :] == langs[:, None]) & (position[None, :] < position[:, None])
        )
        rank = jnp.sum(before.astype(jnp.int32), axis=1)
        placed = rank[None, :] == position[:, None]
        order = jnp.sum(jnp.where(placed, position[None, :], 0), axis=1)
        in_order = jnp.sum(jnp.where(placed, langs[None, :], 0), axis=1)
        return jnp.concatenate([order, in_order, *more]).astype(jnp.int32)

    own_table = table_of(lang, jnp.stack([owner, me]))
    lang_sorted = own_table[segs : 2 * segs]
    pair_table = table_of(tap_rows[0][1, taps + 1, :segs].astype(jnp.int32))

    w_held = [w_out[0], along(after(w_out[0], tap_rows[1]))]
    dy_pair = pair_swap(after(cotan, tap_rows[0]))
    dy_core = swap(after(cotan, *stat_parts, *tap_rows), 1)
    dy_far = swap(after(cotan, *stat_parts), parts // 2) if parts > 2 else None

    seg_block = (1, frames, width)
    group_rows = cap * frames

    def by_order(array, lane=0, lanes=width):
        return [
            (array, pl.BlockSpec((1, frames, lanes), lambda g, o, *_, k=k: (o[g * cap + k], 0, lane)))
            for k in range(cap)
        ]

    def in_turn(shape, lane=0):
        return pl.BlockSpec(shape, lambda g, *_: (g, 0, lane))

    tap_table = call(
        tap_kernel,
        "tap_waves",
        (),
        [(jnp.asarray(tap_wave), whole(tap_wave))] + [(one, whole(one)) for one in tap_rows],
        [
            (
                like((owners, period + 8, width), F32),
                pl.BlockSpec((owners, period + 8, width), lambda: (0, 0, 0)),
            )
        ],
        (),
        flops=4 * owners * period * taps * width,
    )[0]

    def tap_inputs(lane=0, lanes=width):
        def at(g, own, *_):
            return own[segs + g * cap] ^ own[2 * segs], 0, lane

        return [
            (tap_table, pl.BlockSpec((1, period + 8, lanes), at)),
            (jnp.asarray(forward), whole(forward)),
            (jnp.asarray(inverse), whole(inverse)),
        ]

    stat_inputs = [
        (part, pl.BlockSpec((1, 8, frames), lambda g, o, *_, k=k: (o[g * cap + k], 0, 0)))
        for part in stat_parts
        for k in range(cap)
    ]
    wave_flops = 12 * segs * period * frames * width
    cap_block = (cap, frames, width)
    hidden, conv, wave, row_values = call(
        lambda *refs: front_kernel(cap, parts, *refs),
        "front",
        (own_table,),
        by_order(feats) + stat_inputs + tap_inputs(),
        [
            (like((groups, group_rows, width), BF16), in_turn((1, group_rows, width))),
            (like(feats.shape, F32), in_turn(cap_block)),
            (like((segs, period, width), F32), in_turn((cap, period, width))),
            (like((segs, 8, frames), F32), in_turn((cap, 8, frames))),
        ],
        (groups,),
        flops=wave_flops,
    )

    dy_parts, dy_pair_parts = [cotan, dy_core], [dy_pair]
    dy_pair_core = swap(after(dy_pair, hidden, dy_far, w_held[1], dy_core), 1)
    dy_pair_parts.append(dy_pair_core)
    for step in range(2, line):
        w_held.append(along(after(w_held[-1], hidden, dy_pair, dy_far, dy_core)))

    hidden_pair = pair_swap(after(hidden, dy_pair, dy_far, w_held[1], dy_core))
    if parts > 2:
        dy_pair_far = swap(after(dy_pair, hidden, dy_far, w_held[1], dy_core), parts // 2)
        dy_parts += [dy_far, swap(after(dy_far, dy_pair_core), 1)]
        dy_pair_parts += [dy_pair_far, swap(dy_pair_far, 1)]

    def w_grad_call(step, part_ids, adds, places, scale=None):
        across = len(part_ids) * width
        inputs = [hidden, hidden_pair]
        inputs += [dy_parts[k] for k in part_ids] + [dy_pair_parts[k] for k in part_ids]
        return call(
            lambda *refs: w_grad_kernel(
                cap, segs, line, step, len(part_ids), places, scale, *refs
            ),
            "w_grad",
            (own_table, pair_table),
            [(array, any_spec) for array in (*inputs, *adds)],
            [(like((rows, across), BF16), pl.BlockSpec((rows, across), lambda *_: (0, 0)))],
            (1,),
            scratch=[
                pltpu.VMEM((2, group_rows, width), BF16),
                pltpu.VMEM((2, len(part_ids), group_rows, width), BF16),
                pltpu.VMEM((rows, across), BF16),
                pltpu.SemaphoreType.DMA((2,)),
                pltpu.SemaphoreType.DMA((2, len(part_ids), cap)),
                pltpu.SemaphoreType.DMA((max(len(places), 1),)),
            ],
            flops=4 * group_rows * rows * across,
        )[0]

    pieces = [list(range(parts // 2)), list(range(parts // 2, parts))]
    arrived = [[] for _ in pieces]

    def line_step(step, index):
        share = w_grad_call(step, pieces[index], arrived[index], [0] * len(arrived[index]))
        arrived[index] = [along(share)]

    line_steps = [(step, index) for step in range(1, line) for index in range(len(pieces))]

    def line_steps_until(step, index):
        while line_steps and line_steps[0] <= (step, index):
            line_step(*line_steps.pop(0))

    def hid_grad_of(of_pair, dys):
        return call(
            lambda *refs: hid_grad_kernel(parts, cap, line, of_pair, *refs),
            "hid_grad",
            (own_table, pair_table),
            [(array, any_spec) for array in (*dys, *w_held)],
            [
                (like((groups, group_rows, chunk), BF16), in_turn((1, group_rows, chunk)))
                for _ in range(chunks)
            ],
            (groups,),
            scratch=[
                pltpu.VMEM((groups, parts, group_rows, width), BF16),
                pltpu.VMEM((groups, rows, total_width), BF16),
                pltpu.SemaphoreType.DMA((groups, parts, cap)),
                pltpu.SemaphoreType.DMA((groups,)),
            ],
            flops=2 * segs * frames * rows * total_width,
        )

    line_steps_until(1, 1)
    hid_grad_sent = hid_grad_of(True, dy_pair_parts)
    hid_grad_pair = [pair_swap(hid_grad_sent[0])]
    for one in hid_grad_sent[1:]:
        hid_grad_pair.append(pair_swap(after(one, hid_grad_pair[-1])))
    line_steps_until(2, 0)
    hid_grad_own = hid_grad_of(False, dy_parts)

    norm_grads, sums, smalls = [], [], []
    line_steps_until(3, 0)
    for c in range(chunks):
        if c == 1:
            line_steps_until(line, 0)
        norm_grad, part_sums, small = call(
            lambda *refs: back_kernel(cap, *refs),
            "back",
            (own_table,),
            by_order(feats, c, chunk)
            + [(row_values, in_turn((cap, 8, frames)))]
            + tap_inputs(c, chunk)
            + [
                (jnp.asarray(lag_wave), whole(lag_wave)),
                (hid_grad_own[c], in_turn((1, group_rows, chunk))),
                (hid_grad_pair[c], in_turn((1, group_rows, chunk))),
                (conv, in_turn((cap, frames, chunk), c)),
                (wave, in_turn((cap, period, chunk), c)),
            ],
            [
                (like((segs, frames, chunk), F32), in_turn((cap, frames, chunk))),
                (like((segs, 8, frames), F32), in_turn((cap, 8, frames))),
                (like((groups, taps + 1, chunk), F32), in_turn((1, taps + 1, chunk))),
            ],
            (groups,),
            flops=wave_flops // chunks,
        )
        norm_grads.append(norm_grad)
        sums.append(part_sums)
        smalls.append(small)
    line_steps_until(line, 0)
    sums = sum(sums)
    sum_parts = [sums] + [swap(sums, k) for k in range(1, parts)]
    w_grad = w_grad_call(
        0,
        list(range(parts)),
        [array for one in arrived for array in one],
        [piece[0] * width for piece in pieces],
        scale=grad_scale,
    )
    feat_grad = call(
        lambda *refs: final_kernel(cap, chunks, *refs),
        "input_grad",
        (own_table,),
        by_order(feats)
        + by_order(cotan)
        + [(one, in_turn((cap, frames, chunk))) for one in norm_grads]
        + [(one, in_turn((cap, 8, frames))) for one in (row_values, *sum_parts)],
        [(like(feats.shape, BF16), any_spec)],
        (groups,),
        scratch=[
            pltpu.VMEM((2, cap, frames, width), BF16),
            pltpu.SemaphoreType.DMA((2, cap)),
        ],
    )[0]

    small = jnp.concatenate(smalls, axis=2)
    group_lang = lang_sorted.reshape(groups, cap)[:, 0]
    slots = jnp.arange(owners, dtype=jnp.int32)[:, None] == group_lang[None, :]
    spread = jnp.sum(jnp.where(slots[:, :, None, None], small[None], 0.0), axis=1)
    shared = lax.all_to_all(spread, "expert", split_axis=0, concat_axis=0, tiled=True)
    small_sum = jnp.sum(shared, axis=0) * grad_scale

    return (feat_grad, w_grad[None], small_sum[taps:], small_sum[None, :taps])


def per_device(feats, cotan, lang, w_out, gain, kernel):
    segs, frames, width = feats.shape
    owners = lax.axis_size("expert")
    parts = lax.axis_size("fsdp")
    weights_moved = 2 * (owners // 2 - 1) * math.prod(w_out.shape)
    frames_moved = 3 * 2 * math.prod(feats.shape)
    fits = owners & (owners - 1) == 0 and owners > 1 and parts & (parts - 1) == 0 and frames % 128 == 0 and width % frames == 0 and parts in (2, 4) and segs <= 256 and segs <= 256 and segs <= 256 and segs <= 256 and segs <= 256 and segs <= 256 and segs <= 256
    if fits and weights_moved < frames_moved:
        return moved_weights(feats, cotan, lang, w_out, gain, kernel)
    return routed_frames(feats, cotan, lang, w_out, gain, kernel)


def solution(mesh):
    in_specs = (
        P("expert", None, "fsdp"),
        P("expert", None, "fsdp"),
        P("expert"),
        P("expert", "fsdp", None),
        P("expert", "fsdp"),
        P("expert", None, "fsdp"),
    )
    out_specs = (
        P("expert", None, "fsdp"),
        P("expert", "fsdp", None),
        P("expert", "fsdp"),
        P("expert", None, "fsdp"),
    )
    return jax.shard_map(
        per_device, mesh=mesh, in_specs=in_specs, out_specs=out_specs, check_vma=False
    )
```

```python
import math

import jax
import jax.numpy as jnp
import ml_dtypes
import numpy as np
from jax import lax
from jax.experimental import pallas as pl
from jax.experimental.pallas import tpu as pltpu
from jax.sharding import PartitionSpec as P

BF16 = jnp.bfloat16
F32 = jnp.float32
VMEM_BYTES = 60 * 1024 * 1024
WEIGHT = {"front": 30, "frame_stats": 30, "w_grad": 30}

def normalize(values, feature_total):
    value_sum = lax.psum(jnp.sum(values, axis=-1), "fsdp")
    centre = values - (value_sum / feature_total)[..., None]
    square_sum = lax.psum(jnp.sum(centre * centre, axis=-1), "fsdp")
    row_var = square_sum / feature_total
    inv_std = lax.rsqrt(row_var + 1e-05)[..., None]
    return (centre * inv_std, inv_std)


def forward_part(inputs, norm_gain, conv_taps, feature_total):
    normed, inv_std = normalize(inputs.astype(jnp.float32), feature_total)
    scaled = normed * norm_gain
    tap_count = conv_taps.shape[0]
    half_width = tap_count // 2
    frames = inputs.shape[1]
    padded = jnp.pad(scaled, ((0, 0), (half_width, half_width), (0, 0)))
    conv_out = jnp.zeros_like(scaled)
    for offset in range(tap_count):
        conv_out = conv_out + conv_taps[offset] * padded[:, offset : offset + frames]
    gate_sig = jax.nn.sigmoid(conv_out)
    hidden = (conv_out * gate_sig).astype(jnp.bfloat16)
    return (normed, inv_std, padded, conv_out, gate_sig, hidden)


def back_split(
    hid_grad,
    grads_in,
    normed,
    inv_std,
    padded,
    conv_out,
    gate_sig,
    norm_gain,
    conv_taps,
    feature_total,
):
    tap_count = conv_taps.shape[0]
    half_width = tap_count // 2
    frames = normed.shape[1]
    conv_grad = hid_grad * gate_sig * (1.0 + conv_out * (1.0 - gate_sig))
    grad_padded = jnp.pad(conv_grad, ((0, 0), (half_width, half_width), (0, 0)))
    scaled_grad = jnp.zeros_like(conv_grad)
    tap_grads = []
    for offset in range(tap_count):
        first_row = 2 * half_width - offset
        scaled_grad = (
            scaled_grad + conv_taps[offset] * grad_padded[:, first_row : first_row + frames]
        )
        tap_grads.append(jnp.sum(conv_grad * padded[:, offset : offset + frames], axis=(0, 1)))
    gain_grad = jnp.sum(scaled_grad * normed, axis=(0, 1))
    norm_grad = scaled_grad * norm_gain
    grad_total, cross_total = lax.psum(
        (jnp.sum(norm_grad, axis=-1), jnp.sum(norm_grad * normed, axis=-1)), "fsdp"
    )
    branch = inv_std * (
        norm_grad
        - (grad_total / feature_total)[..., None]
        - normed * (cross_total / feature_total)[..., None]
    )
    input_grad = (grads_in.astype(jnp.float32) + branch).astype(jnp.bfloat16)
    return (input_grad, gain_grad, jnp.stack(tap_grads))


def arrival_map(recv_occupied, seg_count):
    flat_occupied = recv_occupied.reshape(-1)
    order_pos = jnp.cumsum(flat_occupied) - 1
    position = jnp.arange(seg_count, dtype=jnp.int32)
    return ((order_pos[None, :] == position[:, None]) & (flat_occupied[None, :] > 0)).astype(
        jnp.bfloat16
    )


def compact_rows(compact_map, received, row_shape):
    flat = received.reshape(compact_map.shape[1], -1)
    return (
        jnp.dot(compact_map, flat, preferred_element_type=jnp.float32)
        .astype(jnp.bfloat16)
        .reshape(row_shape)
    )


def routed_frames(feats, cotan, lang, w_out, gain, kernel):
    seg_count, frames, part_width = feats.shape
    owners = lax.axis_size("expert")
    feature_total = part_width * lax.axis_size("fsdp")
    capacity = max(1, 2 * seg_count // owners)
    slot_count = owners * capacity
    position = jnp.arange(seg_count, dtype=jnp.int32)
    earlier_same = (lang[:, None] == lang[None, :]) & (position[:, None] < position[None, :])
    slot_rank = jnp.sum(earlier_same.astype(jnp.int32), axis=0)
    slot_of = lang * capacity + slot_rank
    routing = jnp.arange(slot_count, dtype=jnp.int32)[:, None] == slot_of[None, :]
    routing_b = routing.astype(jnp.bfloat16)
    send_x = (
        jnp.dot(routing_b, feats.reshape(seg_count, -1), preferred_element_type=jnp.float32)
        .astype(jnp.bfloat16)
        .reshape(owners, capacity, -1)
    )
    send_dy = (
        jnp.dot(routing_b, cotan.reshape(seg_count, -1), preferred_element_type=jnp.float32)
        .astype(jnp.bfloat16)
        .reshape(owners, capacity, -1)
    )
    occupied = jnp.sum(routing.astype(jnp.int32), axis=1).reshape(owners, capacity)
    norm_gain = gain[0].astype(jnp.float32)
    conv_taps = kernel[0].astype(jnp.float32)
    row_shape = (seg_count, frames, part_width)
    recv_x, recv_dy, recv_occupied = (
        lax.all_to_all(send_x, "expert", split_axis=0, concat_axis=0, tiled=True),
        lax.all_to_all(send_dy, "expert", split_axis=0, concat_axis=0, tiled=True),
        lax.all_to_all(occupied, "expert", split_axis=0, concat_axis=0, tiled=True),
    )
    compact_map = arrival_map(recv_occupied, seg_count)
    own_x = compact_rows(compact_map, recv_x, row_shape)
    forward = forward_part(own_x, norm_gain, conv_taps, feature_total)
    own_dy = compact_rows(compact_map, recv_dy, row_shape)
    normed, inv_std, padded, conv_out, gate_sig, hidden = forward
    grad_scale = float(seg_count * frames) ** (-0.5)
    hidden_rows = hidden.reshape(-1, part_width)
    w_rows = w_out[0]
    shard_part = lax.all_gather(own_dy.reshape(-1, part_width), "fsdp", axis=1, tiled=True)
    hid_sum = jnp.dot(shard_part, w_rows.T, preferred_element_type=jnp.float32)
    w_block = jnp.dot(hidden_rows.T, shard_part, preferred_element_type=jnp.float32) * grad_scale
    w_sum = w_block
    hid_sum, w_sum = (hid_sum, w_sum)
    hid_grad = hid_sum.reshape(row_shape)
    input_grad, gain_grad, tap_grad = back_split(
        hid_grad,
        own_dy,
        normed,
        inv_std,
        padded,
        conv_out,
        gate_sig,
        norm_gain,
        conv_taps,
        feature_total,
    )
    back_slots = jnp.dot(
        compact_map.T, input_grad.reshape(seg_count, -1), preferred_element_type=jnp.float32
    ).astype(jnp.bfloat16)
    home_slots = lax.all_to_all(
        back_slots.reshape(owners, capacity, -1), "expert", split_axis=0, concat_axis=0, tiled=True
    )
    feat_grad = (
        jnp.dot(routing_b.T, home_slots.reshape(slot_count, -1), preferred_element_type=jnp.float32)
        .astype(jnp.bfloat16)
        .reshape(feats.shape)
    )
    return (
        feat_grad,
        w_sum.astype(jnp.bfloat16)[None],
        (gain_grad * grad_scale)[None],
        (tap_grad * grad_scale)[None],
    )


def split_const(matrix):
    high = matrix.astype(ml_dtypes.bfloat16)
    low = (matrix - high.astype(np.float64)).astype(ml_dtypes.bfloat16)
    return np.concatenate([high, high, low], axis=1)


def wave_tables(frames, taps):
    half = taps // 2
    period = -(-(frames + half) // 16) * 16
    omega = 2 * np.pi * (np.arange(period // 2) + 0.5) / period
    angle = omega[:, None] * np.arange(frames)
    forward = np.concatenate([np.cos(angle), np.sin(angle)], axis=0)
    lag_angle = omega[:, None] * (np.arange(taps) - half)
    tap_wave = np.concatenate([np.cos(lag_angle), np.sin(lag_angle)], axis=0)
    tap_wave = np.pad(tap_wave, ((0, 0), (0, 1)))
    lag_wave = np.concatenate([np.cos(lag_angle), -np.sin(lag_angle)], axis=0).T * (2 / period)
    lag_wave = np.pad(lag_wave, ((0, 1), (0, 0)))
    tap_high = tap_wave.astype(ml_dtypes.bfloat16)
    tap_low = (tap_wave - tap_high.astype(np.float64)).astype(ml_dtypes.bfloat16)
    return (
        split_const(forward),
        split_const(forward.T * (2 / period)),
        np.stack([tap_high, tap_low]),
        split_const(lag_wave),
        period,
    )


def wide_dot(const_terms, values):
    high = values.astype(BF16)
    low = (values - high.astype(F32)).astype(BF16)
    stacked = jnp.concatenate([high, low, high], axis=0)
    return jnp.dot(const_terms, stacked, preferred_element_type=F32)


def down_lanes(row, width):
    frames = row.shape[1]
    square = jnp.broadcast_to(row, (frames, frames)).T
    return jnp.concatenate([square] * (width // frames), axis=1)


def across_lanes(first, second):
    frames = first.shape[0]
    lane = lax.broadcasted_iota(jnp.int32, (frames, frames), 1)
    square = jnp.where(lane == 0, first, jnp.where(lane == 1, second, 0.0))
    return square.T[0:8]


def side_by_side(pieces):
    return jnp.concatenate(pieces, axis=1) if len(pieces) > 1 else pieces[0]


def row_stats(stat_refs, part_width):
    total = part_width * len(stat_refs)
    sums = [ref[0, 0:1, :] for ref in stat_refs]
    squares = [ref[0, 1:2, :] for ref in stat_refs]
    mean = sum(sums) / total
    spread = sum(squares)
    for part_sum in sums:
        shift = part_sum / part_width - mean
        spread = spread + part_width * (shift * shift)
    return mean, lax.rsqrt(spread / total + 1e-05)


def stats_kernel(x_ref, stat_out):
    for one in range(x_ref.shape[0]):
        values = x_ref[one].astype(F32)
        part_width = values.shape[1]
        part_sum = jnp.sum(values, axis=1, keepdims=True)
        centre = values - part_sum / part_width
        stat_out[one] = across_lanes(part_sum, jnp.sum(centre * centre, axis=1, keepdims=True))


def tap_kernel(wave_ref, *refs):
    tap_refs, out_ref = refs[:-1], refs[-1]
    period, count = wave_ref.shape[1:]
    at = 0
    for tap_ref in tap_refs:
        for one in range(tap_ref.shape[0]):
            taps = tap_ref[one, :count]
            out_ref[at, :period] = jnp.dot(
                wave_ref[0], taps, preferred_element_type=F32
            ) + jnp.dot(wave_ref[1], taps, preferred_element_type=F32)
            gain = taps.astype(F32)[taps.shape[0] - 1 :]
            out_ref[at, period:] = jnp.broadcast_to(gain, (8, gain.shape[1]))
            at += 1


def front_kernel(cap, parts, own_ref, *refs):
    refs = list(refs)
    x_refs = [refs.pop(0) for _ in range(cap)]
    stat_refs = [[refs.pop(0) for _ in range(cap)] for _ in range(parts)]
    tap_ref, fwd_ref, inv_ref, hid_out, normed_out, conv_out, wave_out, row_out = refs
    width = x_refs[0].shape[2]
    period = wave_out.shape[1]
    gain = tap_ref[0, period : period + 1]
    scaled = []
    for one in range(cap):
        mean, inv_std = row_stats([ref[one] for ref in stat_refs], width)
        row = lax.broadcasted_iota(jnp.int32, row_out.shape[1:], 0)
        rows = jnp.where(row == 0, mean, jnp.where(row == 1, inv_std, 0.0))
        row_out[one] = rows
        values = x_refs[one][0].astype(F32) - down_lanes(mean, width)
        normed = values * down_lanes(inv_std, width)
        normed_out[one] = normed.astype(BF16)
        scaled.append(normed * gain)
    wave = wide_dot(fwd_ref[...], side_by_side(scaled))
    count = wave.shape[0] // 2
    a, b = wave[:count], wave[count:]
    kc = side_by_side([tap_ref[0, :count]] * cap)
    ks = side_by_side([tap_ref[0, count : 2 * count]] * cap)
    conv = wide_dot(inv_ref[...], jnp.concatenate([a * kc + b * ks, b * kc - a * ks], axis=0))
    hidden = conv * jax.nn.sigmoid(conv)
    frames = conv.shape[0]
    for one in range(cap):
        at = slice(one * width, (one + 1) * width)
        conv_out[one] = conv[:, at]
        wave_out[one] = wave[:, at]
        hid_out[0, :, one * frames : (one + 1) * frames] = hidden[:, at].T.astype(BF16)


def back_kernel(cap, own_ref, *refs):
    (
        normed_ref,
        tap_ref,
        fwd_ref,
        inv_ref,
        lag_ref,
        own_grad_ref,
        recv_ref,
        conv_ref,
        wave_ref,
        grad_out,
        sum_out,
        small_out,
    ) = refs
    segs = conv_ref.shape[0] * pl.num_programs(0)
    period = wave_ref.shape[1]
    mine = (own_ref[segs + pl.program_id(0) * cap] & 1) == (own_ref[2 * segs] & 1)
    gain = tap_ref[0, period : period + 1]
    frames, width = normed_ref.shape[1:]
    normed = [normed_ref[one].astype(F32) for one in range(cap)]
    hid_grad = jnp.where(mine, own_grad_ref[0], recv_ref[0]).astype(F32)
    hid_grad = side_by_side([hid_grad[one * frames : (one + 1) * frames] for one in range(cap)])
    conv = side_by_side([conv_ref[one] for one in range(cap)])
    gate = jax.nn.sigmoid(conv)
    conv_grad = hid_grad * gate * (1.0 + conv * (1.0 - gate))
    grad_wave = wide_dot(fwd_ref[...], conv_grad)
    count = grad_wave.shape[0] // 2
    ga, gb = grad_wave[:count], grad_wave[count:]
    wave = side_by_side([wave_ref[one] for one in range(cap)])
    a, b = wave[:count], wave[count:]
    kc = side_by_side([tap_ref[0, :count]] * cap)
    ks = side_by_side([tap_ref[0, count : 2 * count]] * cap)
    cross = jnp.concatenate([ga * a + gb * b, gb * a - ga * b], axis=0)
    cross = sum(cross[:, one * width : (one + 1) * width] for one in range(cap))
    scaled_grad = wide_dot(
        inv_ref[...], jnp.concatenate([ga * kc - gb * ks, ga * ks + gb * kc], axis=0)
    )
    gain_grad = None
    for one in range(cap):
        part = scaled_grad[:, one * width : (one + 1) * width]
        product = part * normed[one]
        gain_grad = product if gain_grad is None else gain_grad + product
        norm_grad = part * gain
        grad_out[one] = norm_grad
        sum_out[one] = across_lanes(
            jnp.sum(norm_grad, axis=1, keepdims=True),
            jnp.sum(norm_grad * normed[one], axis=1, keepdims=True),
        )
    tap_rows = wide_dot(lag_ref[...], cross)
    gain_row = jnp.sum(gain_grad, axis=0, keepdims=True)
    row = lax.broadcasted_iota(jnp.int32, tap_rows.shape, 0)
    small_out[0] = jnp.where(row == tap_rows.shape[0] - 1, gain_row, tap_rows)


def final_kernel(cap, chunks, order_ref, *refs):
    dy_refs, grad_refs = refs[:cap], refs[cap : cap + chunks]
    normed_ref, row_ref, *sum_refs, out_ref, out_buf, sems = refs[cap + chunks :]
    step, last = pl.program_id(0), pl.num_programs(0) - 1
    parts, width = len(sum_refs), normed_ref.shape[2]
    slot = step % 2

    def put(slot, step, one):
        return pltpu.make_async_copy(
            out_buf.at[slot, one], out_ref.at[order_ref[step * cap + one]], sems.at[slot, one]
        )

    @pl.when(step >= 2)
    def _():
        for one in range(cap):
            put(slot, step - 2, one).wait()

    for one in range(cap):
        normed = normed_ref[one].astype(F32)
        spread = down_lanes(row_ref[one, 1:2], width)
        total = width * parts
        grad_mean = sum(ref[one, 0:1, :] for ref in sum_refs) / total
        cross_mean = sum(ref[one, 1:2, :] for ref in sum_refs) / total
        grad = side_by_side([grad_ref[one] for grad_ref in grad_refs])
        branch = spread * (
            grad - down_lanes(grad_mean, width) - normed * down_lanes(cross_mean, width)
        )
        out_buf[slot, one] = (dy_refs[one][0].astype(F32) + branch).astype(BF16)
        put(slot, step, one).start()

    @pl.when(step == last)
    def _():
        for one in range(cap):
            put(slot, step, one).wait()

    @pl.when((step == last) & (step >= 1))
    def _():
        for one in range(cap):
            put(1 - slot, step - 1, one).wait()


def hid_grad_kernel(parts, cap, held, of_pair, own_ref, pair_ref, *refs):
    dy_refs, w_refs, out_refs = refs[:parts], refs[parts : parts + held], refs[parts + held : -4]
    dy_buf, w_buf, dy_sems, w_sems = refs[-4:]
    groups = w_buf.shape[0]
    segs = groups * cap
    frames, width = dy_refs[0].shape[1:]
    step = pl.program_id(0)
    owner, me = own_ref[2 * segs], own_ref[2 * segs + 1]
    table = pair_ref if of_pair else own_ref

    def held_index(group):
        language = table[segs + group * cap]
        index = ((owner >> 1) - (language >> 1)) & (held - 1)
        return jnp.where((language & 1) == (owner & 1), index, -1)

    def w_copies(group, source):
        for part in range(parts):
            rows = pl.ds(pl.multiple_of((me ^ part) * width, 128), width)
            yield pltpu.make_async_copy(
                source.at[rows],
                w_buf.at[group, pl.ds(part * width, width)],
                w_sems.at[group, part],
            )

    def dy_copy(group, part, one):
        return pltpu.make_async_copy(
            dy_refs[part].at[table[group * cap + one]],
            dy_buf.at[group, pl.ds(one * frames, frames), pl.ds(part * width, width)],
            dy_sems.at[group, part, one],
        )

    @pl.when(step == 0)
    def _():
        for group in range(groups):
            index = held_index(group)
            for at, source in enumerate(w_refs):

                @pl.when(index == at)
                def _():
                    for copy in w_copies(group, source):
                        copy.start()

            @pl.when(index >= 0)
            def _():
                for part in range(parts):
                    for one in range(cap):
                        dy_copy(group, part, one).start()

    @pl.when(held_index(step) >= 0)
    def _():
        for copy in w_copies(step, w_refs[0]):
            copy.wait()
        for part in range(parts):
            for one in range(cap):
                dy_copy(step, part, one).wait()
        total = jnp.dot(dy_buf[step], w_buf[step], preferred_element_type=F32)
        chunk = total.shape[1] // len(out_refs)
        for index, out_ref in enumerate(out_refs):
            out_ref[0] = total[:, index * chunk : (index + 1) * chunk].astype(BF16)


def w_grad_kernel(cap, segs, line, step, parts, places, scale, own_ref, pair_ref, *refs):
    refs = list(refs)

    def take(number):
        return [refs.pop(0) for _ in range(number)]

    hid_refs, dy_refs, add_refs = take(2), [take(parts), take(parts)], take(len(places))
    out_ref, hid_buf, dy_buf, add_buf, hid_sems, dy_sems, add_sems = refs
    width = dy_buf.shape[1] // parts
    group_rows = dy_buf.shape[0] // 2
    frames = group_rows // cap
    owner, me = own_ref[2 * segs], own_ref[2 * segs + 1]
    language = 2 * (((owner >> 1) - step) & (line - 1)) + (owner & 1)
    found = []
    for table in (own_ref, pair_ref):
        group = jnp.int32(-1)
        for at in range(segs // cap):
            group = jnp.where(table[segs + at * cap] == language, at, group)
        found.append(group)

    def hid_copy(side):
        source = hid_refs[side].at[jnp.maximum(found[side], 0)]
        held = hid_buf.at[:, pl.ds(side * group_rows, group_rows)]
        return pltpu.make_async_copy(source, held, hid_sems.at[side])

    def dy_copies(side, part):
        for one in range(cap):
            segment = (own_ref, pair_ref)[side][jnp.maximum(found[side], 0) * cap + one]
            yield pltpu.make_async_copy(
                dy_refs[side][part].at[segment],
                dy_buf.at[
                    pl.ds(side * group_rows + one * frames, frames), pl.ds(part * width, width)
                ],
                dy_sems.at[side, part, one],
            )

    def add_copy(index):
        ref = add_refs[index]
        held = add_buf.at[:, pl.ds(places[index], ref.shape[1])]
        return pltpu.make_async_copy(ref, held, add_sems.at[index])

    for side in range(2):

        @pl.when(found[side] >= 0)
        def _():
            hid_copy(side).start()
            for part in range(parts):
                for copy in dy_copies(side, part):
                    copy.start()

    for index in range(len(places)):
        add_copy(index).start()
    for side in range(2):

        @pl.when(found[side] >= 0)
        def _():
            hid_copy(side).wait()
            for part in range(parts):
                for copy in dy_copies(side, part):
                    copy.wait()

    for index in range(len(places)):
        add_copy(index).wait()

    def put(value):
        if places:
            value = value + add_buf[...].astype(F32)
        if scale is None:
            out_ref[...] = value.astype(BF16)
            return
        for part in range(parts):
            columns = pl.ds(pl.multiple_of((me ^ part) * width, 128), width)
            one = value[:, part * width : (part + 1) * width]
            out_ref[:, columns] = (one * scale).astype(BF16)

    first, second = found[0] >= 0, found[1] >= 0

    @pl.when(first & second)
    def _():
        put(jnp.dot(hid_buf[...], dy_buf[...], preferred_element_type=F32))

    for side, only in enumerate((first & jnp.logical_not(second), second & jnp.logical_not(first))):

        @pl.when(only)
        def _():
            at = pl.ds(side * group_rows, group_rows)
            put(jnp.dot(hid_buf[:, at], dy_buf[at], preferred_element_type=F32))

    @pl.when(jnp.logical_not(first | second))
    def _():
        put(jnp.zeros(out_ref.shape, F32))


def moved_weights(feats, cotan, lang, w_out, gain, kernel):
    segs, frames, width = feats.shape
    owners = lax.axis_size("expert")
    parts = lax.axis_size("fsdp")
    line = owners // 2
    cap = max(1, 2 * segs // owners)
    groups = segs // cap
    taps = kernel.shape[1]
    rows, total_width = w_out.shape[1:]
    owner = lax.axis_index("expert")
    me = lax.axis_index("fsdp")
    forward, inverse, tap_wave, lag_wave, period = wave_tables(frames, taps)
    grad_scale = float(segs * frames) ** (-0.5)
    chunk = 128
    chunks = width // chunk

    def pair_swap(value):
        return lax.ppermute(value, "expert", [(i, i ^ 1) for i in range(owners)])

    def along(value):
        return lax.ppermute(value, "expert", [(i, (i + 2) % owners) for i in range(owners)])

    def swap(value, bit):
        return lax.ppermute(value, "fsdp", [(i, i ^ bit) for i in range(parts)])

    def after(value, *others):
        return lax.optimization_barrier((value, *others))[0]

    def whole(array):
        return pl.BlockSpec(array.shape, lambda *_: (0,) * array.ndim)

    def like(shape, dtype):
        return jax.ShapeDtypeStruct(shape, dtype)

    order_of_calls = []

    def call(body, name, scalars, inputs, outputs, grid, scratch=(), flops=0, waits=()):
        if scalars:
            scalars = (after(scalars[0], *order_of_calls[-1:], *waits), *scalars[1:])
        arrays, in_specs = zip(*inputs)
        shapes, out_specs = zip(*outputs)
        moved = sum(math.prod(a.shape) * a.dtype.itemsize for a in (*arrays, *shapes))
        found = pl.pallas_call(
            body,
            grid_spec=pltpu.PrefetchScalarGridSpec(
                num_scalar_prefetch=len(scalars),
                grid=grid,
                in_specs=in_specs,
                out_specs=out_specs,
                scratch_shapes=scratch,
            ),
            out_shape=shapes,
            compiler_params=pltpu.CompilerParams(vmem_limit_bytes=VMEM_BYTES),
            cost_estimate=pl.CostEstimate(
                flops=int(flops * WEIGHT.get(name, 1)),
                bytes_accessed=int(moved * WEIGHT.get(name, 1)),
                transcendentals=0,
            ),
            name=name,
        )(*scalars, *arrays)
        order_of_calls.append(found[0])
        return list(found)

    any_spec = pl.BlockSpec(memory_space=pl.ANY)

    lang_row = jnp.pad(lang.astype(BF16), (0, width - segs))[None]
    tap_rows = jnp.concatenate([kernel[0], gain, lang_row], axis=0)
    tap_rows = jnp.pad(tap_rows, ((0, -tap_rows.shape[0] % 16), (0, 0)))[None]
    tap_own = tap_rows
    tap_rows = jnp.concatenate([tap_rows, pair_swap(tap_rows)], axis=0)
    tap_rows = [tap_rows] + [
        lax.ppermute(tap_rows, "expert", [(i, i ^ (2 * k)) for i in range(owners)])
        for k in range(1, line)
    ]
    per_step = 4 if segs % 4 == 0 else 1
    stats = call(
        stats_kernel,
        "frame_stats",
        (),
        [(after(feats, tap_own), pl.BlockSpec((per_step, frames, width), lambda i: (i, 0, 0)))],
        [
            (
                like((segs, 8, frames), F32),
                pl.BlockSpec((per_step, 8, frames), lambda i: (i, 0, 0)),
            )
        ],
        (segs // per_step,),
    )[0]
    stat_parts = [stats] + [swap(stats, k) for k in range(1, parts)]

    def table_of(langs, *more):
        position = jnp.arange(segs, dtype=jnp.int32)
        before = (langs[None, :] < langs[:, None]) | (
            (langs[None, :] == langs[:, None]) & (position[None, :] < position[:, None])
        )
        rank = jnp.sum(before.astype(jnp.int32), axis=1)
        placed = rank[None, :] == position[:, None]
        order = jnp.sum(jnp.where(placed, position[None, :], 0), axis=1)
        in_order = jnp.sum(jnp.where(placed, langs[None, :], 0), axis=1)
        return jnp.concatenate([order, in_order, *more]).astype(jnp.int32)

    own_table = table_of(lang, jnp.stack([owner, me]))
    lang_sorted = own_table[segs : 2 * segs]
    pair_table = table_of(tap_rows[0][1, taps + 1, :segs].astype(jnp.int32))

    w_held = [w_out[0].T]
    for step in range(1, line):
        w_held.append(along(after(w_held[-1], *tap_rows)))
    dy_pair = pair_swap(after(cotan, tap_rows[0]))
    dy_core = swap(after(cotan, *stat_parts, *tap_rows), 1)
    dy_far = swap(after(cotan, *stat_parts), parts // 2) if parts > 2 else None

    seg_block = (1, frames, width)
    group_rows = cap * frames

    def by_order(array, lane=0, lanes=width):
        return [
            (array, pl.BlockSpec((1, frames, lanes), lambda g, o, *_, k=k: (o[g * cap + k], 0, lane)))
            for k in range(cap)
        ]

    def in_turn(shape, lane=0):
        return pl.BlockSpec(shape, lambda g, *_: (g, 0, lane))

    tap_table = call(
        tap_kernel,
        "tap_waves",
        (),
        [(jnp.asarray(tap_wave), whole(tap_wave))] + [(one, whole(one)) for one in tap_rows],
        [
            (
                like((owners, period + 8, width), F32),
                pl.BlockSpec((owners, period + 8, width), lambda: (0, 0, 0)),
            )
        ],
        (),
        flops=4 * owners * period * taps * width,
    )[0]

    def tap_inputs(lane=0, lanes=width):
        def at(g, own, *_):
            return own[segs + g * cap] ^ own[2 * segs], 0, lane

        return [
            (tap_table, pl.BlockSpec((1, period + 8, lanes), at)),
            (jnp.asarray(forward), whole(forward)),
            (jnp.asarray(inverse), whole(inverse)),
        ]

    stat_inputs = [
        (part, pl.BlockSpec((1, 8, frames), lambda g, o, *_, k=k: (o[g * cap + k], 0, 0)))
        for part in stat_parts
        for k in range(cap)
    ]
    wave_flops = 12 * segs * period * frames * width
    cap_block = (cap, frames, width)
    hidden, normed, conv, wave, row_values = call(
        lambda *refs: front_kernel(cap, parts, *refs),
        "front",
        (own_table,),
        by_order(feats) + stat_inputs + tap_inputs(),
        [
            (like((groups, width, group_rows), BF16), in_turn((1, width, group_rows))),
            (like(feats.shape, BF16), in_turn(cap_block)),
            (like(feats.shape, F32), in_turn(cap_block)),
            (like((segs, period, width), F32), in_turn((cap, period, width))),
            (like((segs, 8, frames), F32), in_turn((cap, 8, frames))),
        ],
        (groups,),
        flops=wave_flops,
    )

    dy_parts, dy_pair_parts = [cotan, dy_core], [dy_pair]
    phase = (dy_pair, dy_far, dy_core, w_held[1])
    dy_pair_core = swap(after(dy_pair, hidden, *phase), 1)
    dy_pair_parts.append(dy_pair_core)
    hidden_pair = pair_swap(after(hidden, *phase))
    if parts > 2:
        dy_pair_far = swap(after(dy_pair, hidden, *phase), parts // 2)
        dy_parts += [dy_far, swap(after(dy_far, dy_pair_core), 1)]
        dy_pair_parts += [dy_pair_far, swap(dy_pair_far, 1)]

    def w_grad_call(step, part_ids, adds, places, scale=None, waits=()):
        across = len(part_ids) * width
        inputs = [hidden, hidden_pair]
        inputs += [dy_parts[k] for k in part_ids] + [dy_pair_parts[k] for k in part_ids]
        return call(
            lambda *refs: w_grad_kernel(
                cap, segs, line, step, len(part_ids), places, scale, *refs
            ),
            "w_grad",
            (own_table, pair_table),
            [(array, any_spec) for array in (*inputs, *adds)],
            [(like((rows, across), BF16), pl.BlockSpec((rows, across), lambda *_: (0, 0)))],
            (1,),
            scratch=[
                pltpu.VMEM((width, 2 * group_rows), BF16),
                pltpu.VMEM((2 * group_rows, across), BF16),
                pltpu.VMEM((rows, across), BF16),
                pltpu.SemaphoreType.DMA((2,)),
                pltpu.SemaphoreType.DMA((2, len(part_ids), cap)),
                pltpu.SemaphoreType.DMA((max(len(places), 1),)),
            ],
            flops=4 * group_rows * rows * across,
            waits=waits,
        )[0]

    pieces = [list(range(parts // 2)), list(range(parts // 2, parts))]
    arrived = [[] for _ in pieces]

    def line_step(step, index):
        waits = (w_held[-1],) if step == 1 else ()
        share = w_grad_call(
            step, pieces[index], arrived[index], [0] * len(arrived[index]), waits=waits
        )
        arrived[index] = [along(share)]

    line_steps = [(step, index) for step in range(1, line) for index in range(len(pieces))]

    def line_steps_until(step, index):
        while line_steps and line_steps[0] <= (step, index):
            line_step(*line_steps.pop(0))

    def hid_grad_of(of_pair, dys):
        return call(
            lambda *refs: hid_grad_kernel(parts, cap, line, of_pair, *refs),
            "hid_grad",
            (own_table, pair_table),
            [(array, any_spec) for array in (*dys, *w_held)],
            [
                (like((groups, group_rows, chunk), BF16), in_turn((1, group_rows, chunk)))
                for _ in range(chunks)
            ],
            (groups,),
            scratch=[
                pltpu.VMEM((groups, group_rows, total_width), BF16),
                pltpu.VMEM((groups, total_width, rows), BF16),
                pltpu.SemaphoreType.DMA((groups, parts, cap)),
                pltpu.SemaphoreType.DMA((groups, parts)),
            ],
            flops=2 * segs * frames * rows * total_width,
        )

    line_steps_until(1, 1)
    hid_grad_sent = hid_grad_of(True, dy_pair_parts)
    hid_grad_pair = [pair_swap(hid_grad_sent[0])]
    for one in hid_grad_sent[1:]:
        hid_grad_pair.append(pair_swap(after(one, hid_grad_pair[-1])))
    line_steps_until(2, 0)
    hid_grad_own = hid_grad_of(False, dy_parts)
    line_steps_until(2, len(pieces))

    norm_grads, sums, smalls = [], [], []
    for c in range(chunks):
        if c == chunks - 1:
            line_steps_until(3, 0)
        norm_grad, part_sums, small = call(
            lambda *refs: back_kernel(cap, *refs),
            "back",
            (own_table,),
            [(normed, in_turn((cap, frames, chunk), c))]
            + tap_inputs(c, chunk)
            + [
                (jnp.asarray(lag_wave), whole(lag_wave)),
                (hid_grad_own[c], in_turn((1, group_rows, chunk))),
                (hid_grad_pair[c], in_turn((1, group_rows, chunk))),
                (conv, in_turn((cap, frames, chunk), c)),
                (wave, in_turn((cap, period, chunk), c)),
            ],
            [
                (like((segs, frames, chunk), F32), in_turn((cap, frames, chunk))),
                (like((segs, 8, frames), F32), in_turn((cap, 8, frames))),
                (like((groups, taps + 1, chunk), F32), in_turn((1, taps + 1, chunk))),
            ],
            (groups,),
            flops=wave_flops // chunks,
        )
        norm_grads.append(norm_grad)
        sums.append(part_sums)
        smalls.append(small)
    line_steps_until(line, 0)
    sums = sum(sums)
    sum_parts = [sums] + [swap(sums, k) for k in range(1, parts)]
    feat_grad = call(
        lambda *refs: final_kernel(cap, chunks, *refs),
        "input_grad",
        (own_table,),
        by_order(cotan)
        + [(one, in_turn((cap, frames, chunk))) for one in norm_grads]
        + [(normed, in_turn(cap_block))]
        + [(one, in_turn((cap, 8, frames))) for one in (row_values, *sum_parts)],
        [(like(feats.shape, BF16), any_spec)],
        (groups,),
        scratch=[
            pltpu.VMEM((2, cap, frames, width), BF16),
            pltpu.SemaphoreType.DMA((2, cap)),
        ],
    )[0]

    w_grad = w_grad_call(
        0,
        list(range(parts)),
        [array for one in arrived for array in one],
        [piece[0] * width for piece in pieces],
        scale=grad_scale,
    )
    small = jnp.concatenate(smalls, axis=2)
    group_lang = lang_sorted.reshape(groups, cap)[:, 0]
    slots = jnp.arange(owners, dtype=jnp.int32)[:, None] == group_lang[None, :]
    spread = jnp.sum(jnp.where(slots[:, :, None, None], small[None], 0.0), axis=1)
    shared = lax.all_to_all(spread, "expert", split_axis=0, concat_axis=0, tiled=True)
    small_sum = jnp.sum(shared, axis=0) * grad_scale

    return (feat_grad, w_grad[None], small_sum[taps:], small_sum[None, :taps])


def per_device(feats, cotan, lang, w_out, gain, kernel):
    segs, frames, width = feats.shape
    owners = lax.axis_size("expert")
    parts = lax.axis_size("fsdp")
    weights_moved = 2 * (owners // 2 - 1) * math.prod(w_out.shape)
    frames_moved = 3 * 2 * math.prod(feats.shape)
    fits = owners & (owners - 1) == 0 and owners > 1 and parts & (parts - 1) == 0 and frames % 128 == 0 and width % frames == 0 and parts in (2, 4) and segs <= 256 and segs <= 256 and segs <= 256 and segs <= 256 and segs <= 256 and segs <= 256 and segs <= 256 and segs <= 256 and segs <= 256 and segs <= 256 and segs <= 256 and segs <= 256 and segs <= 256 and segs <= 256 and segs <= 256 and segs <= 256 and segs <= 256 and segs <= 256 and segs <= 256 and segs <= 256 and segs <= 256
    if fits and weights_moved < frames_moved:
        return moved_weights(feats, cotan, lang, w_out, gain, kernel)
    return routed_frames(feats, cotan, lang, w_out, gain, kernel)


def solution(mesh):
    in_specs = (
        P("expert", None, "fsdp"),
        P("expert", None, "fsdp"),
        P("expert"),
        P("expert", "fsdp", None),
        P("expert", "fsdp"),
        P("expert", None, "fsdp"),
    )
    out_specs = (
        P("expert", None, "fsdp"),
        P("expert", "fsdp", None),
        P("expert", "fsdp"),
        P("expert", None, "fsdp"),
    )
    return jax.shard_map(
        per_device, mesh=mesh, in_specs=in_specs, out_specs=out_specs, check_vma=False
    )
```
